32 devices in a mesh: gx: 4 (over z), gy: 4 (over x, core), gz: 2 (over y).
Axes of the slice: x: 2, y: 2, z: 4, core: 2. Of those that a mesh axis runs over, the one named last changes fastest.
Arguments:
- phases: float32 [16, 16, 2, 96, 256], P('gx', 'gy', 'gz'), may hold values from -3.140625 to 3.140625
- diag_tiles: float32 [16, 16, 2, 96, 96], P('gx', 'gy', 'gz'), may hold values from -0.078125 to 0.078125
- local_tiles: float32 [4, 4, 2, 48, 96, 96], P('gx', 'gy', 'gz'), may hold values from -0.078125 to 0.078125
- local_pairs: int32 [4, 4, 2, 2, 48], P('gx', 'gy', 'gz'), may hold values from 0 to 15
- face_tiles: float32 [4, 4, 2, 2, 8, 96, 96], P('gx', 'gy', 'gz'), may hold values from -0.078125 to 0.078125
- face_pairs: int32 [4, 4, 2, 2, 2, 8], P('gx', 'gy', 'gz'), may hold values from 0 to 3
- layer_tiles: float32 [4, 4, 2, 32, 96, 96], P('gx', 'gy', 'gz'), may hold values from -0.078125 to 0.078125
- layer_pairs: int32 [4, 4, 2, 2, 32], P('gx', 'gy', 'gz'), may hold values from 0 to 15
Outputs:
- order_three: float32 [16, 16, 2, 96, 256], P('gx', 'gy', 'gz')
- moments: float32 [2, 7, 256], P('gz')
The draws below stay inside these ranges and needn't reach their ends.
Inputs may be any that keep to these rules, and one draw needn't show every extreme that they name: `local_pairs`: local pairs may repeat and may name one cluster twice. `face_pairs`: face slots number clusters along the face.
All inputs are finite; a program needn't handle non-finite values.
Results may differ from the reference program's by a relative error of at most 0.00005.
Values sent between devices are 32-bit elements; how exact they have to be, the bound alone decides.
A program may use at most 128 MiB of HBM per device.

```python
import math
import jax
import jax.numpy as jnp
from jax import lax

DOF = 96
COLS = 256
SIDE = 4
LOCAL = 48
FACE = 8
LAYER = 32
NX = 16
NY = 16
NZ = 2
N_GX = 4
N_GY = 4
N_GZ = 2


def set_ends(values, key, smallest, top_value):
    longest = values.shape.index(max(values.shape))
    spots = []
    for shift in (0, 1):
        where = [jax.random.randint(jax.random.fold_in(key, axis), (), 0, length) for axis, length in enumerate(values.shape)]
        where[longest] = (where[longest] + shift) % values.shape[longest]
        spots.append(tuple(where))
    return values.at[spots[0]].set(smallest).at[spots[1]].set(top_value)


def levels(stream_key, extent, shards, least, high):
    gain, own = 1.0, jax.random.fold_in(stream_key, 6)
    for position, shards_of in shards:
        steps = jnp.exp(jax.random.uniform(jax.random.fold_in(own, position), (shards_of,), jnp.float32, least / len(shards), high / len(shards)))
        gain = gain * jnp.repeat(steps, extent[position] // shards_of).reshape([-1 if axis == position else 1 for axis in range(len(extent))])
    return gain


def centred(own_key, extent, width, most, split=(), kind=jnp.bfloat16):
    values = jax.random.normal(own_key, extent, jnp.float32) * width
    if len(split) > 0:
        values = levels(own_key, extent, split, -0.22, 0.18) * values
    return jnp.clip(values, min=-most, max=most).astype(kind)


def setup_inputs(seed: int = 0) -> dict:
    seeds = jax.random.split(jax.random.key(seed), 9)
    phases = jnp.clip(jax.random.uniform(seeds[0], (NX, NY, NZ, DOF, COLS), jnp.float32, -3.140625, 3.140625), -3.140625, 3.140625)
    diag_tiles = centred(seeds[1], (NX, NY, NZ, DOF, DOF), (64 * DOF) ** -0.5, 0.078125, ((0, 4), (1, 4), (2, 2)), jnp.float32)
    local_tiles = centred(seeds[2], (N_GX, N_GY, N_GZ, LOCAL, DOF, DOF), (64 * DOF) ** -0.5, 0.078125, ((0, 4), (1, 4), (2, 2)), jnp.float32)
    local_pairs = set_ends(jax.random.randint(seeds[3], (N_GX, N_GY, N_GZ, 2, LOCAL), 0, SIDE * SIDE), jax.random.fold_in(seeds[3], 1), 0, (SIDE * SIDE) - 1).astype(jnp.int32)
    face_tiles = centred(seeds[4], (N_GX, N_GY, N_GZ, 2, FACE, DOF, DOF), (64 * DOF) ** -0.5, 0.078125, ((0, 4), (1, 4), (2, 2)), jnp.float32)
    face_pairs = set_ends(jax.random.randint(seeds[5], (N_GX, N_GY, N_GZ, 2, 2, FACE), 0, SIDE), jax.random.fold_in(seeds[5], 1), 0, SIDE - 1).astype(jnp.int32)
    layer_tiles = centred(seeds[6], (N_GX, N_GY, N_GZ, LAYER, DOF, DOF), (64 * DOF) ** -0.5, 0.078125, ((0, 4), (1, 4), (2, 2)), jnp.float32)
    layer_pairs = set_ends(jax.random.randint(seeds[7], (N_GX, N_GY, N_GZ, 2, LAYER), 0, SIDE * SIDE), jax.random.fold_in(seeds[7], 1), 0, (SIDE * SIDE) - 1).astype(jnp.int32)
    return dict(phases=phases, diag_tiles=diag_tiles, local_tiles=local_tiles, local_pairs=local_pairs, face_tiles=face_tiles, face_pairs=face_pairs, layer_tiles=layer_tiles, layer_pairs=layer_pairs)


TOP_PRECISION = lax.Precision.HIGHEST

def to_bricks(field, trailing):
    shaped = field.reshape((N_GX, SIDE, N_GY, SIDE, N_GZ) + trailing)
    return shaped.transpose(0, 2, 4, 1, 3, 5, 6)

def from_bricks(bricks):
    return bricks.transpose(0, 3, 1, 4, 2, 5, 6).reshape(N_GX * SIDE, N_GY * SIDE, N_GZ, DOF, COLS)

def pair_terms(packed):
    tile_set, pair_list, owner_site_vectors, partner_site_vectors = packed
    forward = jnp.einsum('kab,kbr->kar', tile_set, partner_site_vectors[pair_list[1]], precision=TOP_PRECISION)
    backward = jnp.einsum('kba,kbr->kar', tile_set, owner_site_vectors[pair_list[0]], precision=TOP_PRECISION)
    owner_add = jnp.zeros_like(owner_site_vectors).at[pair_list[0]].add(forward)
    partner_add = jnp.zeros_like(partner_site_vectors).at[pair_list[1]].add(backward)
    return (owner_add, partner_add)

def mapped(tile_set, pair_list, owner_site_vectors, partner_site_vectors):
    brick_count = N_GX * N_GY * N_GZ
    packed = (tile_set.reshape((brick_count,) + tile_set.shape[3:]), pair_list.reshape((brick_count,) + pair_list.shape[3:]), owner_site_vectors.reshape((brick_count,) + owner_site_vectors.shape[3:]), partner_site_vectors.reshape((brick_count,) + partner_site_vectors.shape[3:]))
    owner_add, partner_add = lax.map(pair_terms, packed)
    return (owner_add.reshape(owner_site_vectors.shape), partner_add.reshape(partner_site_vectors.shape))

def operate(field, diag_tiles, local_tiles, local_pairs, face_tiles, face_pairs, layer_tiles, layer_pairs):
    bricks = to_bricks(field, (DOF, COLS))
    diagonal = to_bricks(diag_tiles, (DOF, DOF))
    symmetric = diagonal + jnp.swapaxes(diagonal, 5, 6)
    result = jnp.einsum('ghipqab,ghipqbr->ghipqar', symmetric, bricks, precision=TOP_PRECISION)
    flat = bricks.reshape(N_GX, N_GY, N_GZ, SIDE * SIDE, DOF, COLS)
    owner_add, partner_add = mapped(local_tiles, local_pairs, flat, flat)
    result = result + (owner_add + partner_add).reshape(bricks.shape)
    upper = bricks[:, :, :, SIDE - 1]
    lower = jnp.roll(bricks[:, :, :, 0], -1, axis=0)
    owner_add, partner_add = mapped(face_tiles[:, :, :, 0], face_pairs[:, :, :, 0], upper, lower)
    result = result.at[:, :, :, SIDE - 1].add(owner_add)
    result = result.at[:, :, :, 0].add(jnp.roll(partner_add, 1, axis=0))
    upper = bricks[:, :, :, :, SIDE - 1]
    lower = jnp.roll(bricks[:, :, :, :, 0], -1, axis=1)
    owner_add, partner_add = mapped(face_tiles[:, :, :, 1], face_pairs[:, :, :, 1], upper, lower)
    result = result.at[:, :, :, :, SIDE - 1].add(owner_add)
    result = result.at[:, :, :, :, 0].add(jnp.roll(partner_add, 1, axis=1))
    above = jnp.roll(flat, -1, axis=2)
    owner_add, partner_add = mapped(layer_tiles, layer_pairs, flat, above)
    result = result + (owner_add + jnp.roll(partner_add, 1, axis=2)).reshape(bricks.shape)
    return from_bricks(result)

def product(left_vec, right_vec):
    return lax.optimization_barrier(jnp.sum(left_vec * right_vec, axis=(0, 1, 3)))

def reference(phases, diag_tiles, local_tiles, local_pairs, face_tiles, face_pairs, layer_tiles, layer_pairs):
    lookup_tables = (diag_tiles, local_tiles, local_pairs, face_tiles, face_pairs, layer_tiles, layer_pairs)
    initial = math.sqrt(2.0) * jnp.cos(phases)
    order_one = operate(initial, *lookup_tables)
    order_two = 2.0 * operate(order_one, *lookup_tables) - initial
    order_three = 2.0 * operate(order_two, *lookup_tables) - order_one
    partials = [product(initial, initial), product(initial, order_one), product(order_one, order_one), product(order_two, order_one), product(order_two, order_two), product(order_three, order_two), product(order_three, order_three)]
    stacked = jnp.stack([partials[0], partials[1], 2.0 * partials[2] - partials[0], 2.0 * partials[3] - partials[1], 2.0 * partials[4] - partials[0], 2.0 * partials[5] - partials[1], 2.0 * partials[6] - partials[0]], axis=1)
    moments = stacked / (N_GX * SIDE * N_GY * SIDE * DOF)
    return (order_three, moments)
```

```python
import math

import jax
import jax.numpy as jnp
from jax import lax
from jax.sharding import PartitionSpec as P

EXACT = lax.Precision.HIGH
CHUNKS = 2


def passed_along(block, axis, distance):
    count = lax.axis_size(axis)
    route = [((i - distance) % count, i) for i in range(count)]
    return lax.ppermute(block, axis, route)


def dense(tiles, pairs, number):
    count, degrees = tiles.shape[0], tiles.shape[-1]
    owner = jax.nn.one_hot(pairs[0], number, dtype=jnp.float32)
    partner = jax.nn.one_hot(pairs[1], number, dtype=jnp.float32)
    weight = jnp.einsum("kq,kp->qpk", owner, partner).reshape(number * number, count)
    block = jnp.dot(weight, tiles.reshape(count, degrees * degrees), precision=EXACT)
    block = block.reshape(number, number, degrees, degrees).transpose(0, 2, 1, 3)
    return block.reshape(number * degrees, number * degrees)


def times(matrix, vectors):
    return jnp.dot(matrix, vectors, precision=EXACT)


def shards(
    phases, diag_tiles, local_tiles, local_pairs, face_tiles, face_pairs, layer_tiles, layer_pairs
):
    edge = phases.shape[0]
    clusters = edge * edge
    degrees, columns = phases.shape[3:]
    rows = clusters * degrees
    layers = lax.axis_size("gz")
    initial = math.sqrt(2.0) * jnp.cos(phases[:, :, 0])
    width = columns // CHUNKS
    start = [initial[..., i * width : (i + 1) * width] for i in range(CHUNKS)]

    def send(field):
        flat = field.reshape(rows, width)
        above = passed_along(flat, "gz", -1)
        below = passed_along(flat, "gz", 1) if layers > 2 else None
        east = passed_along(field[0].reshape(edge * degrees, width), "gx", -1)
        west = passed_along(field[edge - 1].reshape(edge * degrees, width), "gx", 1)
        north = passed_along(field[:, 0].reshape(edge * degrees, width), "gy", -1)
        south = passed_along(field[:, edge - 1].reshape(edge * degrees, width), "gy", 1)
        return above, below, east, west, north, south

    first_sent = [send(field) for field in start]

    above_set, above_pairs = layer_tiles[0, 0, 0], layer_pairs[0, 0, 0]
    below_set = passed_along(above_set, "gz", 1)
    below_pairs = passed_along(above_pairs, "gz", 1)
    faces, face_places = face_tiles[0, 0, 0], face_pairs[0, 0, 0]
    west_set = passed_along(faces[0], "gx", 1)
    west_pairs = passed_along(face_places[0], "gx", 1)
    south_set = passed_along(faces[1], "gy", 1)
    south_pairs = passed_along(face_places[1], "gy", 1)

    half = dense(
        jnp.concatenate([local_tiles[0, 0, 0], diag_tiles.reshape(clusters, degrees, degrees)]),
        jnp.concatenate(
            [local_pairs[0, 0, 0], jnp.broadcast_to(jnp.arange(clusters), (2, clusters))], axis=1
        ),
        clusters,
    )
    local_block = half + half.T
    back_set = below_set.transpose(0, 2, 1)
    back_pairs = below_pairs[::-1]
    if layers > 2:
        above_block = dense(above_set, above_pairs, clusters)
        below_block = dense(back_set, back_pairs, clusters)
    else:
        above_block = dense(
            jnp.concatenate([above_set, back_set]),
            jnp.concatenate([above_pairs, back_pairs], axis=1),
            clusters,
        )
    east_block = dense(faces[0], face_places[0], edge)
    north_block = dense(faces[1], face_places[1], edge)
    west_block = dense(west_set.transpose(0, 2, 1), west_pairs[::-1], edge)
    south_block = dense(south_set.transpose(0, 2, 1), south_pairs[::-1], edge)

    def operate(field, sent):
        above, below, east, west, north, south = sent
        result = times(local_block, field.reshape(rows, width)) + times(above_block, above)
        if below is not None:
            result = result + times(below_block, below)
        result = result.reshape(edge, edge, degrees, width)
        line = (edge, degrees, width)
        result = result.at[edge - 1].add(times(east_block, east).reshape(line))
        result = result.at[0].add(times(west_block, west).reshape(line))
        result = result.at[:, edge - 1].add(times(north_block, north).reshape(line))
        result = result.at[:, 0].add(times(south_block, south).reshape(line))
        return result

    def product(left, right):
        return jnp.sum(left * right, axis=(0, 1, 2))

    one = [operate(field, sent) for field, sent in zip(start, first_sent)]
    one_sent = [send(field) for field in one]
    two = [2.0 * operate(f, s) - p for f, s, p in zip(one, one_sent, start)]
    two_sent = [send(field) for field in two]
    three = [2.0 * operate(f, s) - p for f, s, p in zip(two, two_sent, one)]

    partials = [
        jnp.stack(
            [
                product(a, a),
                product(a, b),
                product(b, b),
                product(c, b),
                product(c, c),
                product(d, c),
                product(d, d),
            ]
        )
        for a, b, c, d in zip(start, one, two, three)
    ]
    partials = lax.psum(jnp.concatenate(partials, axis=1), ("gx", "gy"))
    normalizer = lax.axis_size("gx") * lax.axis_size("gy") * rows
    moments = jnp.concatenate(
        [
            partials[:2],
            2.0 * partials[2:] - jnp.stack([partials[i % 2] for i in range(5)]),
        ]
    )
    order_three = jnp.concatenate(three, axis=-1)
    return order_three[:, :, None], (moments / normalizer)[None]


def solution(mesh):
    in_specs = (
        P("gx", "gy", "gz", None, None),
        P("gx", "gy", "gz", None, None),
        P("gx", "gy", "gz", None, None, None),
        P("gx", "gy", "gz", None, None),
        P("gx", "gy", "gz", None, None, None, None),
        P("gx", "gy", "gz", None, None, None),
        P("gx", "gy", "gz", None, None, None),
        P("gx", "gy", "gz", None, None),
    )
    out_specs = (P("gx", "gy", "gz", None, None), P("gz", None, None))
    return jax.shard_map(shards, mesh=mesh, in_specs=in_specs, out_specs=out_specs, check_vma=False)
```

```python
import functools
import math

import jax
import jax.numpy as jnp
from jax import lax
from jax.experimental import pallas as pl
from jax.experimental.pallas import tpu as pltpu
from jax.sharding import PartitionSpec as P

CHUNKS = 2
MESH = pl.DeviceIdType.MESH
VMEM_LIMIT = 60 * 1024 * 1024


def passed_along(block, axis, distance):
    count = lax.axis_size(axis)
    route = [((i - distance) % count, i) for i in range(count)]
    return lax.ppermute(block, axis, route)


def halves(values):
    high = values.astype(jnp.bfloat16)
    return high, (values - high.astype(jnp.float32)).astype(jnp.bfloat16)


def build_kernel(plan, edge, *refs):
    n_src = 1 + max(source for _, parts in plan for source, _ in parts)
    pairs, tiles = refs[:n_src], refs[n_src : 2 * n_src]
    outs = refs[2 * n_src : 2 * n_src + len(plan)]
    block, wide, turn = refs[2 * n_src + len(plan) :]
    degrees, slab = wide.shape
    wide[...] = jnp.zeros_like(wide)
    turn[...] = jnp.zeros_like(turn)

    def place(row, column, span, values):
        wide[:, 0 : values.shape[1]] = values
        group, slot = column // edge, column % edge
        moved = pltpu.roll(wide[...], slot * degrees, 1)
        start = pl.multiple_of(group * slab, slab)
        block[row, :, pl.ds(start, slab)] += moved

    for out, (clusters, parts) in zip(outs, plan):
        span = clusters * degrees

        def clear(i, carry):
            block[i, :, 0:span] = jnp.zeros((degrees, span), jnp.float32)
            return carry

        lax.fori_loop(0, clusters, clear, 0)
        for source, kind in parts:

            def one(k, carry, source=source, kind=kind):
                if kind == "diagonal":
                    first, second = k, k
                else:
                    first, second = pairs[source][0, k], pairs[source][1, k]
                tile = tiles[source][k]
                if kind != "reverse":
                    place(first, second, span, tile)
                if kind != "forward":
                    turn[0:degrees, 0:degrees] = tile
                    place(second, first, span, turn[...].T[0:degrees])
                return carry

            lax.fori_loop(0, tiles[source].shape[0], one, 0)

        def write(i, carry, out=out, span=span):
            high, low = halves(block[i, :, 0:span])
            group, at = i // edge, pl.multiple_of((i % edge) * degrees, degrees)
            out[group, pl.ds(at, degrees), :] = high
            out[group, pl.ds(slab + at, degrees), :] = low
            return carry

        lax.fori_loop(0, clusters, write, 0)


def build(plan, edge, pairs, tiles):
    degrees = tiles[0].shape[-1]
    slab = edge * degrees
    most = max(clusters for clusters, _ in plan)
    around = -(-degrees // 128) * 128
    return pl.pallas_call(
        functools.partial(build_kernel, plan, edge),
        out_shape=[
            jax.ShapeDtypeStruct((c // edge, 2 * slab, c * degrees), jnp.bfloat16) for c, _ in plan
        ],
        in_specs=[pl.BlockSpec(memory_space=pltpu.SMEM)] * len(pairs)
        + [pl.BlockSpec(memory_space=pltpu.VMEM)] * len(tiles),
        out_specs=[pl.BlockSpec(memory_space=pltpu.VMEM)] * len(plan),
        scratch_shapes=[
            pltpu.VMEM((most, degrees, most * degrees), jnp.float32),
            pltpu.VMEM((degrees, slab), jnp.float32),
            pltpu.VMEM((around, around), jnp.float32),
        ],
        compiler_params=pltpu.CompilerParams(vmem_limit_bytes=VMEM_LIMIT),
        cost_estimate=pl.CostEstimate(flops=10**7, bytes_accessed=10**7, transcendentals=0),
    )(*pairs, *tiles)


def recur_kernel(layers, width_x, width_y, normalizer, *refs):
    ways = min(layers - 1, 2)
    field0, first_layer = refs[0], refs[1 : 1 + ways]
    first_faces, refs = refs[1 + ways : 5 + ways], refs[5 + ways :]
    own, across, sides, refs = refs[0], refs[1 : 1 + ways], refs[1 + ways : 5 + ways], refs[5 + ways :]
    out, moments, field1, field2, field3, got_layer, got_face, refs = *refs[:7], refs[7:]
    split, split_side, partial, got_y, got_x, send_sem, recv_sem, sum_send, sum_recv = refs
    chunks, edge, _, degrees, width = field0.shape
    slab = edge * degrees
    fields = [field0, field1, field2, field3]
    me_x, me_y, me_z = lax.axis_index("gx"), lax.axis_index("gy"), lax.axis_index("gz")
    x_peers = [{"gx": lax.rem(me_x + d, width_x)} for d in range(1, width_x)]
    y_peers = [{"gy": lax.rem(me_y + d, width_y)} for d in range(1, width_y)]
    below = {"gz": lax.rem(me_z + layers - 1, layers)}
    above = {"gz": lax.rem(me_z + 1, layers)}
    z_peers = [below, above][:ways]

    barrier = pltpu.get_barrier_semaphore()
    for peer in x_peers + y_peers + z_peers:
        pl.semaphore_signal(barrier, inc=1, device_id=peer, device_id_type=MESH)
    pl.semaphore_wait(barrier, len(x_peers) + len(y_peers) + ways)

    def copies(op, ch):
        field = fields[op + 1]
        found = []
        for j in range(ways):
            found.append((field.at[ch], got_layer.at[op, j, ch], z_peers[j]))
        ends = [
            (field.at[ch, 0], x_peers[-1]),
            (field.at[ch, edge - 1], x_peers[0]),
            (field.at[ch, :, 0], y_peers[-1]),
            (field.at[ch, :, edge - 1], y_peers[0]),
        ]
        for j, (source, peer) in enumerate(ends):
            found.append((source, got_face.at[op, j, ch], peer))
        order = found[ways:] + found[:ways]
        return [
            pltpu.make_async_remote_copy(
                src_ref=source,
                dst_ref=target,
                send_sem=send_sem.at[op, ch, j],
                recv_sem=recv_sem.at[op, ch, j],
                device_id=peer,
                device_id_type=MESH,
            )
            for j, (source, target, peer) in enumerate(order)
        ]

    def into_split(values, i):
        high, low = halves(values.reshape(slab, width))
        split[pl.ds(pl.multiple_of(i * slab, slab), slab), 0:width] = high
        split[pl.ds(pl.multiple_of(i * slab, slab), slab), width : 2 * width] = low

    def folded(both):
        four = both[0:slab] + both[slab : 2 * slab]
        return four[:, 0:width] + four[:, width : 2 * width]

    def apply(matrix, source, target, ch, fresh):
        def fill(i, carry):
            into_split(source(i), i)
            return carry

        lax.fori_loop(0, edge, fill, 0)

        def part(i, carry):
            both = jnp.dot(matrix[i], split[...], preferred_element_type=jnp.float32)
            value = folded(both).reshape(edge, degrees, width)
            target[ch, i] = value if fresh else target[ch, i] + value
            return carry

        lax.fori_loop(0, edge, part, 0)

    def side(j, values):
        high, low = halves(values.reshape(slab, width))
        split_side[:, 0:width] = high
        split_side[:, width : 2 * width] = low
        both = jnp.dot(sides[j][0], split_side[...], preferred_element_type=jnp.float32)
        return folded(both).reshape(edge, degrees, width)

    def inner(left, right, ch):
        def add(i, total):
            return total + jnp.sum(
                (left[ch, i] * right[ch, i]).reshape(slab, width), axis=0, keepdims=True
            )

        return lax.fori_loop(0, edge, add, jnp.zeros((1, width), jnp.float32))

    partial[...] = jnp.zeros_like(partial)
    for op in range(3):
        field, target = fields[op], fields[op + 1]

        def step(ch, carry, op=op, field=field, target=target):
            apply(own, lambda i: field[ch, i], target, ch, True)
            if op > 0:
                for copy in copies(op - 1, ch):
                    copy.wait_recv()
            for j in range(ways):
                if op == 0:
                    apply(across[j], lambda i: first_layer[j][ch, i], target, ch, False)
                else:
                    apply(across[j], lambda i: got_layer[op - 1, j, ch, i], target, ch, False)
            face = [
                first_faces[j][ch] if op == 0 else got_face[op - 1, j, ch] for j in range(4)
            ]
            target[ch, edge - 1] += side(0, face[0])
            target[ch, 0] += side(1, face[1])
            target[ch, :, edge - 1] += side(2, face[2])
            target[ch, :, 0] += side(3, face[3])
            if op > 0:

                def combine(i, carry):
                    target[ch, i] = 2.0 * target[ch, i] - fields[op - 1][ch, i]
                    return carry

                lax.fori_loop(0, edge, combine, 0)
            if op < 2:
                for copy in copies(op, ch):
                    copy.start()
            if op == 0:
                partial[ch, 0:1] = inner(field, field, ch)
            partial[ch, 2 * op + 1 : 2 * op + 2] = inner(target, field, ch)
            partial[ch, 2 * op + 2 : 2 * op + 3] = inner(target, target, ch)
            return carry

        lax.fori_loop(0, chunks, step, 0)

    def gather(stage, peers, slots):
        sends = [
            pltpu.make_async_remote_copy(
                src_ref=partial.at[:],
                dst_ref=slots.at[d],
                send_sem=sum_send.at[stage, d],
                recv_sem=sum_recv.at[stage, d],
                device_id=peer,
                device_id_type=MESH,
            )
            for d, peer in enumerate(peers)
        ]
        for send in sends:
            send.start()
        return sends

    sends = gather(0, y_peers, got_y)
    for ch in range(chunks):
        out[:, :, 0, :, ch * width : (ch + 1) * width] = field3[ch]
    for send in sends:
        send.wait()
    total = partial[...]
    for d in range(len(y_peers)):
        total = total + got_y[d]
    partial[...] = total
    sends = gather(1, x_peers, got_x)
    for send in sends:
        send.wait()
    total = partial[...]
    for d in range(len(x_peers)):
        total = total + got_x[d]
    total = total * (1.0 / normalizer)
    for ch in range(chunks):
        at = slice(ch * width, (ch + 1) * width)
        for k in range(7):
            row = total[ch, k : k + 1]
            if k > 1:
                row = 2.0 * row - total[ch, k % 2 : k % 2 + 1]
            moments[0, k : k + 1, at] = row

    for op in range(2):

        def finish(ch, carry, op=op):
            for copy in copies(op, ch):
                copy.wait_send()
            return carry

        lax.fori_loop(0, chunks, finish, 0)


def recur(field, layer_fields, face_fields, own, across, sides, out_shape, normalizer):
    chunks, edge, _, degrees, width = field.shape
    layers, nx, ny = lax.axis_size("gz"), lax.axis_size("gx"), lax.axis_size("gy")
    ways = len(layer_fields)
    operands = [field, *layer_fields, *face_fields, own, *across, *sides]
    f32 = jnp.float32
    rows = edge * edge * degrees
    return pl.pallas_call(
        functools.partial(recur_kernel, layers, nx, ny, normalizer),
        out_shape=[
            jax.ShapeDtypeStruct(out_shape, f32),
            jax.ShapeDtypeStruct((1, 7, chunks * width), f32),
        ],
        in_specs=[pl.BlockSpec(memory_space=pltpu.VMEM)] * len(operands),
        out_specs=[pl.BlockSpec(memory_space=pltpu.VMEM)] * 2,
        scratch_shapes=[
            pltpu.VMEM(field.shape, f32),
            pltpu.VMEM(field.shape, f32),
            pltpu.VMEM(field.shape, f32),
            pltpu.VMEM((2, ways) + field.shape, f32),
            pltpu.VMEM((2, 4, chunks, edge, degrees, width), f32),
            pltpu.VMEM((rows, 2 * width), jnp.bfloat16),
            pltpu.VMEM((edge * degrees, 2 * width), jnp.bfloat16),
            pltpu.VMEM((chunks, 8, width), f32),
            pltpu.VMEM((ny - 1, chunks, 8, width), f32),
            pltpu.VMEM((nx - 1, chunks, 8, width), f32),
            pltpu.SemaphoreType.DMA((2, chunks, ways + 4)),
            pltpu.SemaphoreType.DMA((2, chunks, ways + 4)),
            pltpu.SemaphoreType.DMA((2, max(nx, ny) - 1)),
            pltpu.SemaphoreType.DMA((2, max(nx, ny) - 1)),
        ],
        compiler_params=pltpu.CompilerParams(
            collective_id=0, has_side_effects=True, vmem_limit_bytes=VMEM_LIMIT
        ),
    )(*operands)


def shards(
    phases, diag_tiles, local_tiles, local_pairs, face_tiles, face_pairs, layer_tiles, layer_pairs
):
    edge = phases.shape[0]
    clusters = edge * edge
    degrees, columns = phases.shape[3:]
    layers = lax.axis_size("gz")
    width = columns // CHUNKS

    own_layer, own_layer_pairs = layer_tiles[0, 0, 0], layer_pairs[0, 0, 0]
    faces, face_places = face_tiles[0, 0, 0], face_pairs[0, 0, 0]
    below_set = passed_along(own_layer, "gz", 1)
    below_pairs = passed_along(own_layer_pairs, "gz", 1)
    west_set = passed_along(faces[0], "gx", 1)
    west_pairs = passed_along(face_places[0], "gx", 1)
    south_set = passed_along(faces[1], "gy", 1)
    south_pairs = passed_along(face_places[1], "gy", 1)

    initial = math.sqrt(2.0) * jnp.cos(phases[:, :, 0])
    field = jnp.stack([initial[..., i * width : (i + 1) * width] for i in range(CHUNKS)])
    layer_fields = [passed_along(field, "gz", -1)]
    if layers > 2:
        layer_fields.append(passed_along(field, "gz", 1))
    face_fields = [
        passed_along(field[:, 0], "gx", -1),
        passed_along(field[:, edge - 1], "gx", 1),
        passed_along(field[:, :, 0], "gy", -1),
        passed_along(field[:, :, edge - 1], "gy", 1),
    ]

    diagonal = diag_tiles.reshape(clusters, degrees, degrees)
    own, east, north = build(
        [
            (clusters, [(0, "both"), (3, "diagonal")]),
            (edge, [(1, "forward")]),
            (edge, [(2, "forward")]),
        ],
        edge,
        [local_pairs[0, 0, 0], face_places[0], face_places[1], face_places[0]],
        [local_tiles[0, 0, 0], faces[0], faces[1], diagonal],
    )
    if layers > 2:
        layer_plan = [(clusters, [(0, "forward")]), (clusters, [(1, "reverse")])]
    else:
        layer_plan = [(clusters, [(0, "forward"), (1, "reverse")])]
    *across, west, south = build(
        layer_plan + [(edge, [(2, "reverse")]), (edge, [(3, "reverse")])],
        edge,
        [own_layer_pairs, below_pairs, west_pairs, south_pairs],
        [own_layer, below_set, west_set, south_set],
    )
    normalizer = lax.axis_size("gx") * lax.axis_size("gy") * clusters * degrees
    order_three, moments = recur(
        field,
        layer_fields,
        face_fields,
        own,
        across,
        [east, west, north, south],
        (edge, edge, 1, degrees, columns),
        float(normalizer),
    )
    return order_three, moments


def solution(mesh):
    in_specs = (
        P("gx", "gy", "gz", None, None),
        P("gx", "gy", "gz", None, None),
        P("gx", "gy", "gz", None, None, None),
        P("gx", "gy", "gz", None, None),
        P("gx", "gy", "gz", None, None, None, None),
        P("gx", "gy", "gz", None, None, None),
        P("gx", "gy", "gz", None, None, None),
        P("gx", "gy", "gz", None, None),
    )
    out_specs = (P("gx", "gy", "gz", None, None), P("gz", None, None))
    return jax.shard_map(shards, mesh=mesh, in_specs=in_specs, out_specs=out_specs, check_vma=False)
```

```python
import functools
import math

import jax
import jax.numpy as jnp
from jax import lax
from jax.experimental import pallas as pl
from jax.experimental.pallas import tpu as pltpu
from jax.sharding import PartitionSpec as P

CHUNKS = 2
TOGETHER = 4
MESH = pl.DeviceIdType.MESH
VMEM_LIMIT = 60 * 1024 * 1024


def passed_along(block, axis, distance):
    count = lax.axis_size(axis)
    route = [((i - distance) % count, i) for i in range(count)]
    return lax.ppermute(block, axis, route)


def halves(values):
    high = values.astype(jnp.bfloat16)
    return high, (values - high.astype(jnp.float32)).astype(jnp.bfloat16)


def packed(tiles):
    count, degrees, _ = tiles.shape
    spare = -degrees % 128
    if spare == 0 or degrees % spare or count * spare % (128 * TOGETHER) or degrees % 8:
        return tiles
    pieces = degrees // spare
    kept = count * degrees // 128
    last = tiles[kept:].reshape(count - kept, degrees, pieces, spare).transpose(0, 2, 1, 3)
    return jnp.concatenate([tiles[:kept], last.reshape(kept, degrees, spare)], axis=2)


def build_kernel(plan, edge, *refs):
    n_src = 1 + max(source for _, parts in plan for source, _ in parts)
    pairs, tiles = refs[:n_src], refs[n_src : 2 * n_src]
    outs = refs[2 * n_src : 2 * n_src + len(plan)]
    block, wide, turn = refs[2 * n_src + len(plan) :]
    _, degrees, slab = wide.shape
    wide[...] = jnp.zeros_like(wide)
    turn[...] = jnp.zeros_like(turn)

    def place(places):
        for j, (_, _, values) in enumerate(places):
            wide[j, :, 0 : values.shape[1]] = values
        moved = [
            pltpu.roll(wide[j], (column % edge) * degrees, 1)
            for j, (_, column, _) in enumerate(places)
        ]
        for (row, column, _), values in zip(places, moved):
            start = pl.multiple_of((column // edge) * slab, slab)
            block[row, :, pl.ds(start, slab)] += values

    def turned(j, tile):
        for at, piece in tile:
            turn[j, 0:degrees, at : at + piece.shape[1]] = piece
        return turn[j].T[0:degrees]

    for out, (clusters, parts) in zip(outs, plan):
        span = clusters * degrees

        def clear(i, carry):
            block[i, :, 0:span] = jnp.zeros((degrees, span), jnp.float32)
            return carry

        lax.fori_loop(0, clusters, clear, 0)
        for source, kind in parts:
            stored = tiles[source]
            spare = stored.shape[2] - degrees

            def some(step, carry, source=source, kind=kind, stored=stored, first_tile=0, tail=False):
                places = []
                for j in range(TOGETHER):
                    k = step * TOGETHER + j
                    index = first_tile + k
                    if kind == "diagonal":
                        owner, partner = k, k
                    else:
                        owner, partner = pairs[source][0, index], pairs[source][1, index]
                    if tail:
                        pieces = degrees // spare
                        tile = [
                            (i * spare, stored[k * pieces + i][:, degrees:]) for i in range(pieces)
                        ]
                    else:
                        tile = [(0, stored[k][:, 0:degrees])]
                    if kind != "reverse":
                        places.append((owner, partner, tile[0][1]))
                    if kind != "forward":
                        places.append((partner, owner, turned(j, tile)))
                place(places)
                return carry

            count = stored.shape[0]
            lax.fori_loop(0, count // TOGETHER, some, 0)
            if spare:
                rest = functools.partial(some, first_tile=count, tail=True)
                lax.fori_loop(0, count * spare // degrees // TOGETHER, rest, 0)

        def write(i, carry, out=out, span=span):
            high, low = halves(block[i, :, 0:span])
            group, at = i // edge, pl.multiple_of((i % edge) * degrees, degrees)
            out[group, pl.ds(at, degrees), :] = high
            out[group, pl.ds(slab + at, degrees), :] = low
            return carry

        lax.fori_loop(0, clusters, write, 0)


def build(plan, edge, pairs, tiles, cost):
    degrees = tiles[0].shape[1]
    slab = edge * degrees
    most = max(clusters for clusters, _ in plan)
    around = -(-degrees // 128) * 128
    return pl.pallas_call(
        functools.partial(build_kernel, plan, edge),
        out_shape=[
            jax.ShapeDtypeStruct((c // edge, 2 * slab, c * degrees), jnp.bfloat16) for c, _ in plan
        ],
        in_specs=[pl.BlockSpec(memory_space=pltpu.SMEM)] * len(pairs)
        + [pl.BlockSpec(memory_space=pltpu.VMEM)] * len(tiles),
        out_specs=[pl.BlockSpec(memory_space=pltpu.VMEM)] * len(plan),
        scratch_shapes=[
            pltpu.VMEM((most, degrees, most * degrees), jnp.float32),
            pltpu.VMEM((2 * TOGETHER, degrees, slab), jnp.float32),
            pltpu.VMEM((TOGETHER, around, around), jnp.float32),
        ],
        compiler_params=pltpu.CompilerParams(vmem_limit_bytes=VMEM_LIMIT),
        cost_estimate=pl.CostEstimate(flops=250 * cost, bytes_accessed=cost, transcendentals=0),
    )(*pairs, *tiles)


def recur_kernel(layers, width_x, width_y, normalizer, *refs):
    ways = min(layers - 1, 2)
    field0, first_layer = refs[0], refs[1 : 1 + ways]
    first_faces, refs = refs[1 + ways : 5 + ways], refs[5 + ways :]
    stored, refs = refs[: 5 + ways], refs[5 + ways :]
    out, moments, field1, field2, field3, got_layer, got_face, refs = *refs[:7], refs[7:]
    loaded, load_sem, refs = refs[: 5 + ways], refs[5 + ways], refs[6 + ways :]
    own, across, sides = loaded[0], loaded[1 : 1 + ways], loaded[1 + ways :]
    split, split_side, partial, got_y, got_x, send_sem, recv_sem, sum_send, sum_recv = refs
    chunks, edge, _, degrees, width = field0.shape
    slab = edge * degrees
    fields = [field0, field1, field2, field3]
    me_x, me_y, me_z = lax.axis_index("gx"), lax.axis_index("gy"), lax.axis_index("gz")
    x_peers = [{"gx": lax.rem(me_x + d, width_x)} for d in range(1, width_x)]
    y_peers = [{"gy": lax.rem(me_y + d, width_y)} for d in range(1, width_y)]
    below = {"gz": lax.rem(me_z + layers - 1, layers)}
    above = {"gz": lax.rem(me_z + 1, layers)}
    z_peers = [below, above][:ways]

    loads = [
        pltpu.make_async_copy(source, target, load_sem.at[j])
        for j, (source, target) in enumerate(zip(stored, loaded))
    ]
    for load in loads:
        load.start()
    barrier = pltpu.get_barrier_semaphore()
    for peer in x_peers + y_peers + z_peers:
        pl.semaphore_signal(barrier, inc=1, device_id=peer, device_id_type=MESH)
    pl.semaphore_wait(barrier, len(x_peers) + len(y_peers) + ways)

    def copies(op, ch):
        field = fields[op]
        found = []
        for j in range(ways):
            found.append((field.at[ch], got_layer.at[op, j, ch], z_peers[j]))
        ends = [
            (field.at[ch, 0], x_peers[-1]),
            (field.at[ch, edge - 1], x_peers[0]),
            (field.at[ch, :, 0], y_peers[-1]),
            (field.at[ch, :, edge - 1], y_peers[0]),
        ]
        for j, (source, peer) in enumerate(ends):
            found.append((source, got_face.at[op, j, ch], peer))
        order = found[ways:] + found[:ways]
        return [
            pltpu.make_async_remote_copy(
                src_ref=source,
                dst_ref=target,
                send_sem=send_sem.at[op, ch, j],
                recv_sem=recv_sem.at[op, ch, j],
                device_id=peer,
                device_id_type=MESH,
            )
            for j, (source, target, peer) in enumerate(order)
        ]

    def into_split(values, i):
        high, low = halves(values.reshape(slab, width))
        split[pl.ds(pl.multiple_of(i * slab, slab), slab), 0:width] = high
        split[pl.ds(pl.multiple_of(i * slab, slab), slab), width : 2 * width] = low

    def folded(both):
        four = both[0:slab] + both[slab : 2 * slab]
        return four[:, 0:width] + four[:, width : 2 * width]

    def apply(matrix, source, target, ch, fresh):
        def fill(i, carry):
            into_split(source(i), i)
            return carry

        lax.fori_loop(0, edge, fill, 0)

        def part(i, carry):
            both = jnp.dot(matrix[i], split[...], preferred_element_type=jnp.float32)
            value = folded(both).reshape(edge, degrees, width)
            target[ch, i] = value if fresh else target[ch, i] + value
            return carry

        lax.fori_loop(0, edge, part, 0)

    def side(j, values):
        high, low = halves(values.reshape(slab, width))
        split_side[:, 0:width] = high
        split_side[:, width : 2 * width] = low
        both = jnp.dot(sides[j][0], split_side[...], preferred_element_type=jnp.float32)
        return folded(both).reshape(edge, degrees, width)

    def inner(left, right, ch):
        def add(i, total):
            return total + jnp.sum(
                (left[ch, i] * right[ch, i]).reshape(slab, width), axis=0, keepdims=True
            )

        return lax.fori_loop(0, edge, add, jnp.zeros((1, width), jnp.float32))

    for ch in range(1, chunks):
        for copy in copies(0, ch):
            copy.start()
    partial[...] = jnp.zeros_like(partial)
    for op in range(3):
        field, target = fields[op], fields[op + 1]

        def step(ch, carry, op=op, field=field, target=target):
            first = op == 0 and isinstance(ch, int) and ch == 0
            if first:
                loads[0].wait()
            apply(own, lambda i: field[ch, i], target, ch, True)
            if first:
                for load in loads[1:]:
                    load.wait()
            else:
                for copy in copies(op, ch):
                    copy.wait_recv()
            for j in range(ways):
                if first:
                    apply(across[j], lambda i: first_layer[j][i], target, ch, False)
                else:
                    apply(across[j], lambda i: got_layer[op, j, ch, i], target, ch, False)
            face = [first_faces[j][...] if first else got_face[op, j, ch] for j in range(4)]
            target[ch, edge - 1] += side(0, face[0])
            target[ch, 0] += side(1, face[1])
            target[ch, :, edge - 1] += side(2, face[2])
            target[ch, :, 0] += side(3, face[3])
            if op > 0:

                def combine(i, carry):
                    target[ch, i] = 2.0 * target[ch, i] - fields[op - 1][ch, i]
                    return carry

                lax.fori_loop(0, edge, combine, 0)
            if op < 2:
                for copy in copies(op + 1, ch):
                    copy.start()
            if op == 0:
                partial[ch, 0:1] = inner(field, field, ch)
            partial[ch, 2 * op + 1 : 2 * op + 2] = inner(target, field, ch)
            partial[ch, 2 * op + 2 : 2 * op + 3] = inner(target, target, ch)
            return carry

        if op == 0:
            for ch in range(chunks):
                step(ch, 0)
        else:
            lax.fori_loop(0, chunks, step, 0)

    def gather(stage, peers, slots):
        sends = [
            pltpu.make_async_remote_copy(
                src_ref=partial.at[:],
                dst_ref=slots.at[d],
                send_sem=sum_send.at[stage, d],
                recv_sem=sum_recv.at[stage, d],
                device_id=peer,
                device_id_type=MESH,
            )
            for d, peer in enumerate(peers)
        ]
        for send in sends:
            send.start()
        return sends

    sends = gather(0, y_peers, got_y)
    for ch in range(chunks):
        out[:, :, 0, :, ch * width : (ch + 1) * width] = field3[ch]
    for send in sends:
        send.wait()
    total = partial[...]
    for d in range(len(y_peers)):
        total = total + got_y[d]
    partial[...] = total
    sends = gather(1, x_peers, got_x)
    for send in sends:
        send.wait()
    total = partial[...]
    for d in range(len(x_peers)):
        total = total + got_x[d]
    total = total * (1.0 / normalizer)
    for ch in range(chunks):
        at = slice(ch * width, (ch + 1) * width)
        for k in range(7):
            row = total[ch, k : k + 1]
            if k > 1:
                row = 2.0 * row - total[ch, k % 2 : k % 2 + 1]
            moments[0, k : k + 1, at] = row

    for op in range(3):

        def finish(ch, carry, op=op):
            for copy in copies(op, ch):
                copy.wait_send()
            return carry

        lax.fori_loop(1 if op == 0 else 0, chunks, finish, 0)


def recur(field, layer_fields, face_fields, own, across, sides, out_shape, normalizer):
    chunks, edge, _, degrees, width = field.shape
    layers, nx, ny = lax.axis_size("gz"), lax.axis_size("gx"), lax.axis_size("gy")
    ways = len(layer_fields)
    operands = [field, *layer_fields, *face_fields, own, *across, *sides]
    f32 = jnp.float32
    rows = edge * edge * degrees
    return pl.pallas_call(
        functools.partial(recur_kernel, layers, nx, ny, normalizer),
        out_shape=[
            jax.ShapeDtypeStruct(out_shape, f32),
            jax.ShapeDtypeStruct((1, 7, chunks * width), f32),
        ],
        in_specs=[pl.BlockSpec(memory_space=pltpu.VMEM)] * (5 + ways)
        + [pl.BlockSpec(memory_space=pl.ANY)] * (5 + ways),
        out_specs=[pl.BlockSpec(memory_space=pltpu.VMEM)] * 2,
        scratch_shapes=[
            pltpu.VMEM(field.shape, f32),
            pltpu.VMEM(field.shape, f32),
            pltpu.VMEM(field.shape, f32),
            pltpu.VMEM((3, ways) + field.shape, f32),
            pltpu.VMEM((3, 4, chunks, edge, degrees, width), f32),
            *[pltpu.VMEM(matrix.shape, matrix.dtype) for matrix in (own, *across, *sides)],
            pltpu.SemaphoreType.DMA((5 + ways,)),
            pltpu.VMEM((rows, 2 * width), jnp.bfloat16),
            pltpu.VMEM((edge * degrees, 2 * width), jnp.bfloat16),
            pltpu.VMEM((chunks, 8, width), f32),
            pltpu.VMEM((ny - 1, chunks, 8, width), f32),
            pltpu.VMEM((nx - 1, chunks, 8, width), f32),
            pltpu.SemaphoreType.DMA((3, chunks, ways + 4)),
            pltpu.SemaphoreType.DMA((3, chunks, ways + 4)),
            pltpu.SemaphoreType.DMA((2, max(nx, ny) - 1)),
            pltpu.SemaphoreType.DMA((2, max(nx, ny) - 1)),
        ],
        compiler_params=pltpu.CompilerParams(
            collective_id=0, has_side_effects=True, vmem_limit_bytes=VMEM_LIMIT
        ),
    )(*operands)


def shards(
    phases, diag_tiles, local_tiles, local_pairs, face_tiles, face_pairs, layer_tiles, layer_pairs
):
    edge = phases.shape[0]
    clusters = edge * edge
    degrees, columns = phases.shape[3:]
    layers = lax.axis_size("gz")
    width = columns // CHUNKS

    own_layer, own_layer_pairs = layer_tiles[0, 0, 0], layer_pairs[0, 0, 0]
    faces, face_places = face_tiles[0, 0, 0], face_pairs[0, 0, 0]
    below_set = passed_along(packed(own_layer), "gz", 1)
    below_pairs = passed_along(own_layer_pairs, "gz", 1)
    west_set = passed_along(faces[0], "gx", 1)
    west_pairs = passed_along(face_places[0], "gx", 1)
    south_set = passed_along(faces[1], "gy", 1)
    south_pairs = passed_along(face_places[1], "gy", 1)

    initial = math.sqrt(2.0) * jnp.cos(phases[:, :, 0])
    field = jnp.stack([initial[..., i * width : (i + 1) * width] for i in range(CHUNKS)])
    layer_fields = [passed_along(field[0], "gz", -1)]
    if layers > 2:
        layer_fields.append(passed_along(field[0], "gz", 1))
    face_fields = [
        passed_along(field[0, 0], "gx", -1),
        passed_along(field[0, edge - 1], "gx", 1),
        passed_along(field[0, :, 0], "gy", -1),
        passed_along(field[0, :, edge - 1], "gy", 1),
    ]

    diagonal = diag_tiles.reshape(clusters, degrees, degrees)
    own, east, north = build(
        [
            (clusters, [(0, "both"), (3, "diagonal")]),
            (edge, [(1, "forward")]),
            (edge, [(2, "forward")]),
        ],
        edge,
        [local_pairs[0, 0, 0], face_places[0], face_places[1], face_places[0]],
        [local_tiles[0, 0, 0], faces[0], faces[1], diagonal],
        6 * 10**7,
    )
    if layers > 2:
        layer_plan = [(clusters, [(0, "forward")]), (clusters, [(1, "reverse")])]
    else:
        layer_plan = [(clusters, [(0, "forward"), (1, "reverse")])]
    *across, west, south = build(
        layer_plan + [(edge, [(2, "reverse")]), (edge, [(3, "reverse")])],
        edge,
        [own_layer_pairs, below_pairs, west_pairs, south_pairs],
        [own_layer, below_set, west_set, south_set],
        3 * 10**7,
    )
    normalizer = lax.axis_size("gx") * lax.axis_size("gy") * clusters * degrees
    order_three, moments = recur(
        field,
        layer_fields,
        face_fields,
        own,
        across,
        [east, west, north, south],
        (edge, edge, 1, degrees, columns),
        float(normalizer),
    )
    return order_three, moments


def solution(mesh):
    in_specs = (
        P("gx", "gy", "gz", None, None),
        P("gx", "gy", "gz", None, None),
        P("gx", "gy", "gz", None, None, None),
        P("gx", "gy", "gz", None, None),
        P("gx", "gy", "gz", None, None, None, None),
        P("gx", "gy", "gz", None, None, None),
        P("gx", "gy", "gz", None, None, None),
        P("gx", "gy", "gz", None, None),
    )
    out_specs = (P("gx", "gy", "gz", None, None), P("gz", None, None))
    return jax.shard_map(shards, mesh=mesh, in_specs=in_specs, out_specs=out_specs, check_vma=False)
```

```python
import functools
import math

import jax
import jax.numpy as jnp
from jax import lax
from jax.experimental import pallas as pl
from jax.experimental.pallas import tpu as pltpu
from jax.sharding import PartitionSpec as P

CHUNKS = 2
TOGETHER = 4
MESH = pl.DeviceIdType.MESH
VMEM_LIMIT = 60 * 1024 * 1024


def passed_along(block, axis, distance):
    count = lax.axis_size(axis)
    route = [((i - distance) % count, i) for i in range(count)]
    return lax.ppermute(block, axis, route)


def halves(values):
    high = values.astype(jnp.bfloat16)
    return high, (values - high.astype(jnp.float32)).astype(jnp.bfloat16)


def packed(tiles):
    count, degrees, _ = tiles.shape
    spare = -degrees % 128
    if spare == 0 or degrees % spare or count * spare % (128 * TOGETHER) or degrees % 8:
        return tiles
    pieces = degrees // spare
    kept = count * degrees // 128
    last = tiles[kept:].reshape(count - kept, degrees, pieces, spare).transpose(0, 2, 1, 3)
    return jnp.concatenate([tiles[:kept], last.reshape(kept, degrees, spare)], axis=2)


def with_pairs(tiles, pairs):
    _, degrees, lanes = tiles.shape
    spare = ((0, degrees - pairs.shape[0]), (0, lanes - pairs.shape[1]))
    return jnp.concatenate([tiles, jnp.pad(pairs.astype(jnp.float32), spare)[None]])


def sent_along(tiles, pairs, axis):
    received = passed_along(with_pairs(tiles, pairs), axis, 1)
    return received, received[-1, 0:2, 0 : pairs.shape[1]].astype(jnp.int32)


def build_kernel(plan, counts, edge, *refs):
    n_src = 1 + max(source for _, parts in plan for source, _ in parts)
    pairs, tiles = refs[:n_src], refs[n_src : 2 * n_src]
    outs = refs[2 * n_src : 2 * n_src + len(plan)]
    block, wide, turn = refs[2 * n_src + len(plan) :]
    _, degrees, slab = wide.shape
    wide[...] = jnp.zeros_like(wide)
    turn[...] = jnp.zeros_like(turn)

    def place(places):
        for j, (_, _, values) in enumerate(places):
            wide[j, :, 0 : values.shape[1]] = values
        moved = [
            pltpu.roll(wide[j], (column % edge) * degrees, 1)
            for j, (_, column, _) in enumerate(places)
        ]
        for (row, column, _), values in zip(places, moved):
            start = pl.multiple_of((column // edge) * slab, slab)
            block[row, :, pl.ds(start, slab)] += values

    def turned(j, tile):
        for at, piece in tile:
            turn[j, 0:degrees, at : at + piece.shape[1]] = piece
        return turn[j].T[0:degrees]

    for out, (clusters, parts) in zip(outs, plan):
        span = clusters * degrees

        def clear(i, carry):
            block[i, :, 0:span] = jnp.zeros((degrees, span), jnp.float32)
            return carry

        lax.fori_loop(0, clusters, clear, 0)
        for source, kind in parts:
            stored = tiles[source]
            spare = stored.shape[2] - degrees

            def some(step, carry, source=source, kind=kind, stored=stored, first_tile=0, tail=False):
                places = []
                for j in range(TOGETHER):
                    k = step * TOGETHER + j
                    index = first_tile + k
                    if kind == "diagonal":
                        owner, partner = k, k
                    else:
                        owner, partner = pairs[source][0, index], pairs[source][1, index]
                    if tail:
                        pieces = degrees // spare
                        tile = [
                            (i * spare, stored[k * pieces + i][:, degrees:]) for i in range(pieces)
                        ]
                    else:
                        tile = [(0, stored[k][:, 0:degrees])]
                    if kind != "reverse":
                        places.append((owner, partner, tile[0][1]))
                    if kind != "forward":
                        places.append((partner, owner, turned(j, tile)))
                place(places)
                return carry

            count = counts[source]
            lax.fori_loop(0, count // TOGETHER, some, 0)
            if spare:
                rest = functools.partial(some, first_tile=count, tail=True)
                lax.fori_loop(0, count * spare // degrees // TOGETHER, rest, 0)

        def write(i, carry, out=out, span=span):
            high, low = halves(block[i, :, 0:span])
            group, at = i // edge, pl.multiple_of((i % edge) * degrees, degrees)
            out[group, pl.ds(at, degrees), :] = high
            out[group, pl.ds(slab + at, degrees), :] = low
            return carry

        lax.fori_loop(0, clusters, write, 0)


def build(plan, counts, edge, pairs, tiles, cost):
    degrees = tiles[0].shape[1]
    slab = edge * degrees
    most = max(clusters for clusters, _ in plan)
    around = -(-degrees // 128) * 128
    return pl.pallas_call(
        functools.partial(build_kernel, plan, counts, edge),
        out_shape=[
            jax.ShapeDtypeStruct((c // edge, 2 * slab, c * degrees), jnp.bfloat16) for c, _ in plan
        ],
        in_specs=[pl.BlockSpec(memory_space=pltpu.SMEM)] * len(pairs)
        + [pl.BlockSpec(memory_space=pltpu.VMEM)] * len(tiles),
        out_specs=[pl.BlockSpec(memory_space=pltpu.VMEM)] * len(plan),
        scratch_shapes=[
            pltpu.VMEM((most, degrees, most * degrees), jnp.float32),
            pltpu.VMEM((2 * TOGETHER, degrees, slab), jnp.float32),
            pltpu.VMEM((TOGETHER, around, around), jnp.float32),
        ],
        compiler_params=pltpu.CompilerParams(vmem_limit_bytes=VMEM_LIMIT),
        cost_estimate=pl.CostEstimate(flops=250 * cost, bytes_accessed=cost, transcendentals=0),
    )(*pairs, *tiles)


def recur_kernel(layers, width_x, width_y, normalizer, *refs):
    ways = min(layers - 1, 2)
    field0, first_layer = refs[0], refs[1 : 1 + ways]
    refs = refs[1 + ways :]
    stored, refs = refs[: 5 + ways], refs[5 + ways :]
    out, moments, field1, field2, field3, got_layer, got_face, refs = *refs[:7], refs[7:]
    loaded, load_sem, refs = refs[: 5 + ways], refs[5 + ways], refs[6 + ways :]
    own, across, sides = loaded[0], loaded[1 : 1 + ways], loaded[1 + ways :]
    split, split_side, partial, got_y, got_x, send_sem, recv_sem, sum_send, sum_recv = refs
    chunks, edge, _, degrees, width = field0.shape
    slab = edge * degrees
    fields = [field0, field1, field2, field3]
    me_x, me_y, me_z = lax.axis_index("gx"), lax.axis_index("gy"), lax.axis_index("gz")
    x_peers = [{"gx": lax.rem(me_x + d, width_x)} for d in range(1, width_x)]
    y_peers = [{"gy": lax.rem(me_y + d, width_y)} for d in range(1, width_y)]
    below = {"gz": lax.rem(me_z + layers - 1, layers)}
    above = {"gz": lax.rem(me_z + 1, layers)}
    z_peers = [below, above][:ways]

    loads = [
        pltpu.make_async_copy(source, target, load_sem.at[j])
        for j, (source, target) in enumerate(zip(stored, loaded))
    ]
    for load in loads:
        load.start()
    barrier = pltpu.get_barrier_semaphore()
    for peer in x_peers + y_peers + z_peers:
        pl.semaphore_signal(barrier, inc=1, device_id=peer, device_id_type=MESH)
    pl.semaphore_wait(barrier, len(x_peers) + len(y_peers) + ways)

    def copies(op, ch):
        field = fields[op]
        found = []
        for j in range(ways):
            found.append((field.at[ch], got_layer.at[op, j, ch], z_peers[j]))
        ends = [
            (field.at[ch, 0], x_peers[-1]),
            (field.at[ch, edge - 1], x_peers[0]),
            (field.at[ch, :, 0], y_peers[-1]),
            (field.at[ch, :, edge - 1], y_peers[0]),
        ]
        for j, (source, peer) in enumerate(ends):
            found.append((source, got_face.at[op, j, ch], peer))
        order = found[ways:] + found[:ways]
        return [
            pltpu.make_async_remote_copy(
                src_ref=source,
                dst_ref=target,
                send_sem=send_sem.at[op, ch, j],
                recv_sem=recv_sem.at[op, ch, j],
                device_id=peer,
                device_id_type=MESH,
            )
            for j, (source, target, peer) in enumerate(order)
        ]

    def into_split(values, i):
        high, low = halves(values.reshape(slab, width))
        split[pl.ds(pl.multiple_of(i * slab, slab), slab), 0:width] = high
        split[pl.ds(pl.multiple_of(i * slab, slab), slab), width : 2 * width] = low

    def folded(both):
        four = both[0:slab] + both[slab : 2 * slab]
        return four[:, 0:width] + four[:, width : 2 * width]

    def apply(matrix, source, target, ch, fresh):
        def fill(i, carry):
            into_split(source(i), i)
            return carry

        lax.fori_loop(0, edge, fill, 0)

        def part(i, carry):
            both = jnp.dot(matrix[i], split[...], preferred_element_type=jnp.float32)
            value = folded(both).reshape(edge, degrees, width)
            target[ch, i] = value if fresh else target[ch, i] + value
            return carry

        lax.fori_loop(0, edge, part, 0)

    def side(j, values):
        high, low = halves(values.reshape(slab, width))
        split_side[:, 0:width] = high
        split_side[:, width : 2 * width] = low
        both = jnp.dot(sides[j][0], split_side[...], preferred_element_type=jnp.float32)
        return folded(both).reshape(edge, degrees, width)

    def inner(left, right, ch):
        def add(i, total):
            return total + jnp.sum(
                (left[ch, i] * right[ch, i]).reshape(slab, width), axis=0, keepdims=True
            )

        return lax.fori_loop(0, edge, add, jnp.zeros((1, width), jnp.float32))

    for ch in range(chunks):
        for copy in copies(0, ch)[: 4 if ch == 0 else None]:
            copy.start()
    partial[...] = jnp.zeros_like(partial)
    for op in range(3):
        field, target = fields[op], fields[op + 1]

        def step(ch, carry, op=op, field=field, target=target):
            first = op == 0 and isinstance(ch, int) and ch == 0
            if first:
                loads[0].wait()
            apply(own, lambda i: field[ch, i], target, ch, True)
            if first:
                for load in loads[1:]:
                    load.wait()
            else:
                for copy in copies(op, ch):
                    copy.wait_recv()
            for j in range(ways):
                if first:
                    apply(across[j], lambda i: first_layer[j][i], target, ch, False)
                else:
                    apply(across[j], lambda i: got_layer[op, j, ch, i], target, ch, False)
            if first:
                for copy in copies(0, 0)[:4]:
                    copy.wait_recv()
            face = [got_face[op, j, ch] for j in range(4)]
            target[ch, edge - 1] += side(0, face[0])
            target[ch, 0] += side(1, face[1])
            target[ch, :, edge - 1] += side(2, face[2])
            target[ch, :, 0] += side(3, face[3])
            if op > 0:

                def combine(i, carry):
                    target[ch, i] = 2.0 * target[ch, i] - fields[op - 1][ch, i]
                    return carry

                lax.fori_loop(0, edge, combine, 0)
            if op < 2:
                for copy in copies(op + 1, ch):
                    copy.start()
            if op == 0:
                partial[ch, 0:1] = inner(field, field, ch)
            partial[ch, 2 * op + 1 : 2 * op + 2] = inner(target, field, ch)
            partial[ch, 2 * op + 2 : 2 * op + 3] = inner(target, target, ch)
            return carry

        if op == 0:
            for ch in range(chunks):
                step(ch, 0)
        else:
            lax.fori_loop(0, chunks, step, 0)

    def gather(stage, peers, slots):
        sends = [
            pltpu.make_async_remote_copy(
                src_ref=partial.at[:],
                dst_ref=slots.at[d],
                send_sem=sum_send.at[stage, d],
                recv_sem=sum_recv.at[stage, d],
                device_id=peer,
                device_id_type=MESH,
            )
            for d, peer in enumerate(peers)
        ]
        for send in sends:
            send.start()
        return sends

    sends = gather(0, y_peers, got_y)
    for ch in range(chunks):
        out[:, :, 0, :, ch * width : (ch + 1) * width] = field3[ch]
    for send in sends:
        send.wait()
    total = partial[...]
    for d in range(len(y_peers)):
        total = total + got_y[d]
    partial[...] = total
    sends = gather(1, x_peers, got_x)
    for send in sends:
        send.wait()
    total = partial[...]
    for d in range(len(x_peers)):
        total = total + got_x[d]
    total = total * (1.0 / normalizer)
    for ch in range(chunks):
        at = slice(ch * width, (ch + 1) * width)
        for k in range(7):
            row = total[ch, k : k + 1]
            if k > 1:
                row = 2.0 * row - total[ch, k % 2 : k % 2 + 1]
            moments[k, :, at] = row

    for copy in copies(0, 0)[:4]:
        copy.wait_send()
    for op in range(3):

        def finish(ch, carry, op=op):
            for copy in copies(op, ch):
                copy.wait_send()
            return carry

        lax.fori_loop(1 if op == 0 else 0, chunks, finish, 0)


def recur(field, layer_fields, own, across, sides, out_shape, normalizer):
    chunks, edge, _, degrees, width = field.shape
    layers, nx, ny = lax.axis_size("gz"), lax.axis_size("gx"), lax.axis_size("gy")
    ways = len(layer_fields)
    operands = [field, *layer_fields, own, *across, *sides]
    f32 = jnp.float32
    rows = edge * edge * degrees
    return pl.pallas_call(
        functools.partial(recur_kernel, layers, nx, ny, normalizer),
        out_shape=[
            jax.ShapeDtypeStruct(out_shape, f32),
            jax.ShapeDtypeStruct((7, 1, chunks * width), f32),
        ],
        in_specs=[pl.BlockSpec(memory_space=pltpu.VMEM)] * (1 + ways)
        + [pl.BlockSpec(memory_space=pl.ANY)] * (5 + ways),
        out_specs=[pl.BlockSpec(memory_space=pltpu.VMEM)] * 2,
        scratch_shapes=[
            pltpu.VMEM(field.shape, f32),
            pltpu.VMEM(field.shape, f32),
            pltpu.VMEM(field.shape, f32),
            pltpu.VMEM((3, ways) + field.shape, f32),
            pltpu.VMEM((3, 4, chunks, edge, degrees, width), f32),
            *[pltpu.VMEM(matrix.shape, matrix.dtype) for matrix in (own, *across, *sides)],
            pltpu.SemaphoreType.DMA((5 + ways,)),
            pltpu.VMEM((rows, 2 * width), jnp.bfloat16),
            pltpu.VMEM((edge * degrees, 2 * width), jnp.bfloat16),
            pltpu.VMEM((chunks, 8, width), f32),
            pltpu.VMEM((ny - 1, chunks, 8, width), f32),
            pltpu.VMEM((nx - 1, chunks, 8, width), f32),
            pltpu.SemaphoreType.DMA((3, chunks, ways + 4)),
            pltpu.SemaphoreType.DMA((3, chunks, ways + 4)),
            pltpu.SemaphoreType.DMA((2, max(nx, ny) - 1)),
            pltpu.SemaphoreType.DMA((2, max(nx, ny) - 1)),
        ],
        compiler_params=pltpu.CompilerParams(
            collective_id=0, has_side_effects=True, vmem_limit_bytes=VMEM_LIMIT
        ),
    )(*operands)


def shards(
    phases, diag_tiles, local_tiles, local_pairs, face_tiles, face_pairs, layer_tiles, layer_pairs
):
    edge = phases.shape[0]
    clusters = edge * edge
    degrees, columns = phases.shape[3:]
    layers = lax.axis_size("gz")
    width = columns // CHUNKS

    own_layer, own_layer_pairs = layer_tiles[0, 0, 0], layer_pairs[0, 0, 0]
    faces, face_places = face_tiles[0, 0, 0], face_pairs[0, 0, 0]
    layer_packed = packed(own_layer)
    below_set, below_pairs = sent_along(layer_packed, own_layer_pairs, "gz")
    west_set, west_pairs = sent_along(faces[0], face_places[0], "gx")
    south_set, south_pairs = sent_along(faces[1], face_places[1], "gy")

    initial = math.sqrt(2.0) * jnp.cos(phases[:, :, 0])
    field = jnp.stack([initial[..., i * width : (i + 1) * width] for i in range(CHUNKS)])
    layer_fields = [passed_along(field[0], "gz", -1)]
    if layers > 2:
        layer_fields.append(passed_along(field[0], "gz", 1))
    diagonal = diag_tiles.reshape(clusters, degrees, degrees)
    own, east, north = build(
        [
            (clusters, [(0, "both"), (3, "diagonal")]),
            (edge, [(1, "forward")]),
            (edge, [(2, "forward")]),
        ],
        [local_tiles.shape[3], faces.shape[1], faces.shape[1], clusters],
        edge,
        [local_pairs[0, 0, 0], face_places[0], face_places[1], face_places[0]],
        [local_tiles[0, 0, 0], faces[0], faces[1], diagonal],
        6 * 10**7,
    )
    if layers > 2:
        layer_plan = [(clusters, [(0, "forward")]), (clusters, [(1, "reverse")])]
    else:
        layer_plan = [(clusters, [(0, "forward"), (1, "reverse")])]
    *across, west, south = build(
        layer_plan + [(edge, [(2, "reverse")]), (edge, [(3, "reverse")])],
        [own_layer.shape[0], layer_packed.shape[0], faces.shape[1], faces.shape[1]],
        edge,
        [own_layer_pairs, below_pairs, west_pairs, south_pairs],
        [own_layer, below_set, west_set, south_set],
        3 * 10**7,
    )
    normalizer = lax.axis_size("gx") * lax.axis_size("gy") * clusters * degrees
    order_three, moments = recur(
        field,
        layer_fields,
        own,
        across,
        [east, west, north, south],
        (edge, edge, 1, degrees, columns),
        float(normalizer),
    )
    return order_three, moments.transpose(1, 0, 2)


def solution(mesh):
    in_specs = (
        P("gx", "gy", "gz", None, None),
        P("gx", "gy", "gz", None, None),
        P("gx", "gy", "gz", None, None, None),
        P("gx", "gy", "gz", None, None),
        P("gx", "gy", "gz", None, None, None, None),
        P("gx", "gy", "gz", None, None, None),
        P("gx", "gy", "gz", None, None, None),
        P("gx", "gy", "gz", None, None),
    )
    out_specs = (P("gx", "gy", "gz", None, None), P("gz", None, None))
    return jax.shard_map(shards, mesh=mesh, in_specs=in_specs, out_specs=out_specs, check_vma=False)
```

```python
import functools
import math

import jax
import jax.numpy as jnp
from jax import lax
from jax.experimental import pallas as pl
from jax.experimental.pallas import tpu as pltpu
from jax.sharding import PartitionSpec as P

CHUNKS = 2
TOGETHER = 4
PIECES = 2
MESH = pl.DeviceIdType.MESH
VMEM_LIMIT = 60 * 1024 * 1024


def passed_along(block, axis, distance):
    count = lax.axis_size(axis)
    route = [((i - distance) % count, i) for i in range(count)]
    return lax.ppermute(block, axis, route)


def halves(values):
    high = values.astype(jnp.bfloat16)
    return high, (values - high.astype(jnp.float32)).astype(jnp.bfloat16)


def packed(tiles):
    count, degrees, _ = tiles.shape
    spare = -degrees % 128
    if spare == 0 or degrees % spare or count * spare % (128 * TOGETHER) or degrees % 8:
        return tiles
    pieces = degrees // spare
    kept = count * degrees // 128
    last = tiles[kept:].reshape(count - kept, degrees, pieces, spare).transpose(0, 2, 1, 3)
    return jnp.concatenate([tiles[:kept], last.reshape(kept, degrees, spare)], axis=2)


def with_pairs(tiles, pairs):
    _, degrees, lanes = tiles.shape
    spare = ((0, degrees - pairs.shape[0]), (0, lanes - pairs.shape[1]))
    return jnp.concatenate([tiles, jnp.pad(pairs.astype(jnp.float32), spare)[None]])


def sent_along(carried, pairs, axis):
    received = passed_along(carried, axis, 1)
    return received, received[-1, 0:2, 0 : pairs.shape[1]].astype(jnp.int32)


def build_kernel(plan, counts, edge, *refs):
    n_src = 1 + max(source for _, parts in plan for source, _ in parts)
    pairs, tiles = refs[:n_src], refs[n_src : 2 * n_src]
    outs = refs[2 * n_src : 2 * n_src + len(plan)]
    block, wide, turn = refs[2 * n_src + len(plan) :]
    _, degrees, slab = wide.shape
    wide[...] = jnp.zeros_like(wide)
    turn[...] = jnp.zeros_like(turn)

    def place(places):
        for j, (_, _, values) in enumerate(places):
            wide[j, :, 0 : values.shape[1]] = values
        moved = [
            pltpu.roll(wide[j], (column % edge) * degrees, 1)
            for j, (_, column, _) in enumerate(places)
        ]
        for (row, column, _), values in zip(places, moved):
            start = pl.multiple_of((column // edge) * slab, slab)
            block[row, :, pl.ds(start, slab)] += values

    def turned(j, tile):
        for at, piece in tile:
            turn[j, 0:degrees, at : at + piece.shape[1]] = piece
        return turn[j].T[0:degrees]

    for out, (clusters, parts) in zip(outs, plan):
        span = clusters * degrees

        def clear(i, carry):
            block[i, :, 0:span] = jnp.zeros((degrees, span), jnp.float32)
            return carry

        lax.fori_loop(0, clusters, clear, 0)
        for source, kind in parts:
            stored = tiles[source]
            spare = stored.shape[2] - degrees

            def some(step, carry, source=source, kind=kind, stored=stored, first_tile=0, tail=False):
                places = []
                for j in range(TOGETHER):
                    k = step * TOGETHER + j
                    index = first_tile + k
                    if kind == "diagonal":
                        owner, partner = k, k
                    else:
                        owner, partner = pairs[source][0, index], pairs[source][1, index]
                    if tail:
                        pieces = degrees // spare
                        tile = [
                            (i * spare, stored[k * pieces + i][:, degrees:]) for i in range(pieces)
                        ]
                    else:
                        tile = [(0, stored[k][:, 0:degrees])]
                    if kind != "reverse":
                        places.append((owner, partner, tile[0][1]))
                    if kind != "forward":
                        places.append((partner, owner, turned(j, tile)))
                place(places)
                return carry

            count = counts[source]
            lax.fori_loop(0, count // TOGETHER, some, 0)
            if spare:
                rest = functools.partial(some, first_tile=count, tail=True)
                lax.fori_loop(0, count * spare // degrees // TOGETHER, rest, 0)

        def write(i, carry, out=out, span=span):
            high, low = halves(block[i, :, 0:span])
            group, at = i // edge, pl.multiple_of((i % edge) * degrees, degrees)
            out[group, pl.ds(at, degrees), :] = high
            out[group, pl.ds(slab + at, degrees), :] = low
            return carry

        lax.fori_loop(0, clusters, write, 0)


def build(plan, counts, edge, pairs, tiles, cost):
    degrees = tiles[0].shape[1]
    slab = edge * degrees
    most = max(clusters for clusters, _ in plan)
    around = -(-degrees // 128) * 128
    return pl.pallas_call(
        functools.partial(build_kernel, plan, counts, edge),
        out_shape=[
            jax.ShapeDtypeStruct((c // edge, 2 * slab, c * degrees), jnp.bfloat16) for c, _ in plan
        ],
        in_specs=[pl.BlockSpec(memory_space=pltpu.SMEM)] * len(pairs)
        + [pl.BlockSpec(memory_space=pltpu.VMEM)] * len(tiles),
        out_specs=[pl.BlockSpec(memory_space=pltpu.VMEM)] * len(plan),
        scratch_shapes=[
            pltpu.VMEM((most, degrees, most * degrees), jnp.float32),
            pltpu.VMEM((2 * TOGETHER, degrees, slab), jnp.float32),
            pltpu.VMEM((TOGETHER, around, around), jnp.float32),
        ],
        compiler_params=pltpu.CompilerParams(vmem_limit_bytes=VMEM_LIMIT),
        cost_estimate=pl.CostEstimate(flops=250 * cost, bytes_accessed=cost, transcendentals=0),
    )(*pairs, *tiles)


def recur_kernel(layers, width_x, width_y, normalizer, *refs):
    ways = min(layers - 1, 2)
    field0, first_layer = refs[0], refs[1 : 1 + ways]
    refs = refs[1 + ways :]
    stored, refs = refs[: 5 + ways], refs[5 + ways :]
    out, moments, field1, field2, field3, got_layer, got_face, refs = *refs[:7], refs[7:]
    loaded, load_sem, refs = refs[: 5 + ways], refs[5 + ways], refs[6 + ways :]
    own, across, sides = loaded[0], loaded[1 : 1 + ways], loaded[1 + ways :]
    split, split_side, partial, got_y, got_x, send_sem, recv_sem, sum_send, sum_recv = refs
    chunks, edge, _, degrees, width = field0.shape
    slab = edge * degrees
    pieces = PIECES if edge % PIECES == 0 else 1
    fields = [field0, field1, field2, field3]
    me_x, me_y, me_z = lax.axis_index("gx"), lax.axis_index("gy"), lax.axis_index("gz")
    x_peers = [{"gx": lax.rem(me_x + d, width_x)} for d in range(1, width_x)]
    y_peers = [{"gy": lax.rem(me_y + d, width_y)} for d in range(1, width_y)]
    below = {"gz": lax.rem(me_z + layers - 1, layers)}
    above = {"gz": lax.rem(me_z + 1, layers)}
    z_peers = [below, above][:ways]

    loads = [
        pltpu.make_async_copy(source, target, load_sem.at[j])
        for j, (source, target) in enumerate(zip(stored, loaded))
    ]
    for load in loads:
        load.start()
    barrier = pltpu.get_barrier_semaphore()
    for peer in x_peers + y_peers + z_peers:
        pl.semaphore_signal(barrier, inc=1, device_id=peer, device_id_type=MESH)
    pl.semaphore_wait(barrier, len(x_peers) + len(y_peers) + ways)

    def copies(op, ch):
        field = fields[op]
        found = []
        for j in range(ways):
            for p in range(pieces):
                piece = pl.ds(p * (edge // pieces), edge // pieces)
                found.append(
                    (field.at[ch, piece], got_layer.at[op, j, ch, piece], z_peers[j])
                )
        ends = [
            (field.at[ch, 0], x_peers[-1]),
            (field.at[ch, edge - 1], x_peers[0]),
            (field.at[ch, :, 0], y_peers[-1]),
            (field.at[ch, :, edge - 1], y_peers[0]),
        ]
        for j, (source, peer) in enumerate(ends):
            found.append((source, got_face.at[op, j, ch], peer))
        order = found[ways * pieces :] + found[: ways * pieces]
        return [
            pltpu.make_async_remote_copy(
                src_ref=source,
                dst_ref=target,
                send_sem=send_sem.at[op, ch, j],
                recv_sem=recv_sem.at[op, ch, j],
                device_id=peer,
                device_id_type=MESH,
            )
            for j, (source, target, peer) in enumerate(order)
        ]

    def into_split(values, i):
        high, low = halves(values.reshape(slab, width))
        split[pl.ds(pl.multiple_of(i * slab, slab), slab), 0:width] = high
        split[pl.ds(pl.multiple_of(i * slab, slab), slab), width : 2 * width] = low

    def folded(both):
        four = both[0:slab] + both[slab : 2 * slab]
        return four[:, 0:width] + four[:, width : 2 * width]

    def apply(matrix, source, target, ch, fresh, begin, end):
        def fill(i, carry):
            into_split(source(i), i)
            return carry

        lax.fori_loop(begin, end, fill, 0)
        rows = slice(begin * slab, end * slab)

        def part(i, carry):
            both = jnp.dot(matrix[i, :, rows], split[rows], preferred_element_type=jnp.float32)
            value = folded(both).reshape(edge, degrees, width)
            target[ch, i] = value if fresh else target[ch, i] + value
            return carry

        lax.fori_loop(0, edge, part, 0)

    def side(j, values):
        high, low = halves(values.reshape(slab, width))
        split_side[:, 0:width] = high
        split_side[:, width : 2 * width] = low
        both = jnp.dot(sides[j][0], split_side[...], preferred_element_type=jnp.float32)
        return folded(both).reshape(edge, degrees, width)

    def inner(left, right, ch):
        def add(i, total):
            return total + jnp.sum(
                (left[ch, i] * right[ch, i]).reshape(slab, width), axis=0, keepdims=True
            )

        return lax.fori_loop(0, edge, add, jnp.zeros((1, width), jnp.float32))

    for ch in range(chunks):
        for copy in copies(0, ch)[: 4 if ch == 0 else None]:
            copy.start()
    partial[...] = jnp.zeros_like(partial)
    for op in range(3):
        field, target = fields[op], fields[op + 1]

        def step(ch, carry, op=op, field=field, target=target):
            first = op == 0 and isinstance(ch, int) and ch == 0
            if first:
                loads[0].wait()
            apply(own, lambda i: field[ch, i], target, ch, True, 0, edge)
            if first:
                for load in loads[1:]:
                    load.wait()
            arrivals = copies(op, ch)
            for copy in arrivals[:4]:
                copy.wait_recv()
            face = [got_face[op, j, ch] for j in range(4)]
            target[ch, edge - 1] += side(0, face[0])
            target[ch, 0] += side(1, face[1])
            target[ch, :, edge - 1] += side(2, face[2])
            target[ch, :, 0] += side(3, face[3])
            for j in range(ways):
                for p in range(pieces):
                    begin, end = p * (edge // pieces), (p + 1) * (edge // pieces)
                    if first:
                        apply(across[j], lambda i: first_layer[j][i], target, ch, False, begin, end)
                    else:
                        arrivals[4 + j * pieces + p].wait_recv()
                        apply(
                            across[j],
                            lambda i: got_layer[op, j, ch, i],
                            target,
                            ch,
                            False,
                            begin,
                            end,
                        )
            if op > 0:

                def combine(i, carry):
                    target[ch, i] = 2.0 * target[ch, i] - fields[op - 1][ch, i]
                    return carry

                lax.fori_loop(0, edge, combine, 0)
            if op < 2:
                for copy in copies(op + 1, ch):
                    copy.start()
            if op == 0:
                partial[ch, 0:1] = inner(field, field, ch)
            partial[ch, 2 * op + 1 : 2 * op + 2] = inner(target, field, ch)
            partial[ch, 2 * op + 2 : 2 * op + 3] = inner(target, target, ch)
            return carry

        if op == 0:
            for ch in range(chunks):
                step(ch, 0)
        else:
            lax.fori_loop(0, chunks, step, 0)

    def gather(stage, peers, slots):
        sends = [
            pltpu.make_async_remote_copy(
                src_ref=partial.at[:],
                dst_ref=slots.at[d],
                send_sem=sum_send.at[stage, d],
                recv_sem=sum_recv.at[stage, d],
                device_id=peer,
                device_id_type=MESH,
            )
            for d, peer in enumerate(peers)
        ]
        for send in sends:
            send.start()
        return sends

    sends = gather(0, y_peers, got_y)
    for ch in range(chunks):
        out[:, :, 0, :, ch * width : (ch + 1) * width] = field3[ch]
    for send in sends:
        send.wait()
    total = partial[...]
    for d in range(len(y_peers)):
        total = total + got_y[d]
    partial[...] = total
    sends = gather(1, x_peers, got_x)
    for send in sends:
        send.wait()
    total = partial[...]
    for d in range(len(x_peers)):
        total = total + got_x[d]
    total = total * (1.0 / normalizer)
    for ch in range(chunks):
        at = slice(ch * width, (ch + 1) * width)
        for k in range(7):
            row = total[ch, k : k + 1]
            if k > 1:
                row = 2.0 * row - total[ch, k % 2 : k % 2 + 1]
            moments[k, :, at] = row

    for copy in copies(0, 0)[:4]:
        copy.wait_send()
    for op in range(3):

        def finish(ch, carry, op=op):
            for copy in copies(op, ch):
                copy.wait_send()
            return carry

        lax.fori_loop(1 if op == 0 else 0, chunks, finish, 0)


def recur(field, layer_fields, own, across, sides, out_shape, normalizer):
    chunks, edge, _, degrees, width = field.shape
    layers, nx, ny = lax.axis_size("gz"), lax.axis_size("gx"), lax.axis_size("gy")
    ways = len(layer_fields)
    operands = [field, *layer_fields, own, *across, *sides]
    f32 = jnp.float32
    rows = edge * edge * degrees
    return pl.pallas_call(
        functools.partial(recur_kernel, layers, nx, ny, normalizer),
        out_shape=[
            jax.ShapeDtypeStruct(out_shape, f32),
            jax.ShapeDtypeStruct((7, 1, chunks * width), f32),
        ],
        in_specs=[pl.BlockSpec(memory_space=pltpu.VMEM)] * (1 + ways)
        + [pl.BlockSpec(memory_space=pl.ANY)] * (5 + ways),
        out_specs=[pl.BlockSpec(memory_space=pltpu.VMEM)] * 2,
        scratch_shapes=[
            pltpu.VMEM(field.shape, f32),
            pltpu.VMEM(field.shape, f32),
            pltpu.VMEM(field.shape, f32),
            pltpu.VMEM((3, ways) + field.shape, f32),
            pltpu.VMEM((3, 4, chunks, edge, degrees, width), f32),
            *[pltpu.VMEM(matrix.shape, matrix.dtype) for matrix in (own, *across, *sides)],
            pltpu.SemaphoreType.DMA((5 + ways,)),
            pltpu.VMEM((rows, 2 * width), jnp.bfloat16),
            pltpu.VMEM((edge * degrees, 2 * width), jnp.bfloat16),
            pltpu.VMEM((chunks, 8, width), f32),
            pltpu.VMEM((ny - 1, chunks, 8, width), f32),
            pltpu.VMEM((nx - 1, chunks, 8, width), f32),
            pltpu.SemaphoreType.DMA((3, chunks, PIECES * ways + 4)),
            pltpu.SemaphoreType.DMA((3, chunks, PIECES * ways + 4)),
            pltpu.SemaphoreType.DMA((2, max(nx, ny) - 1)),
            pltpu.SemaphoreType.DMA((2, max(nx, ny) - 1)),
        ],
        compiler_params=pltpu.CompilerParams(
            collective_id=0, has_side_effects=True, vmem_limit_bytes=VMEM_LIMIT
        ),
    )(*operands)


def shards(
    phases, diag_tiles, local_tiles, local_pairs, face_tiles, face_pairs, layer_tiles, layer_pairs
):
    edge = phases.shape[0]
    clusters = edge * edge
    degrees, columns = phases.shape[3:]
    layers = lax.axis_size("gz")
    width = columns // CHUNKS

    own_layer, own_layer_pairs = layer_tiles[0, 0, 0], layer_pairs[0, 0, 0]
    faces, face_places = face_tiles[0, 0, 0], face_pairs[0, 0, 0]
    layer_packed = packed(own_layer)
    carried = with_pairs(layer_packed, own_layer_pairs)
    below_set, below_pairs = sent_along(carried, own_layer_pairs, "gz")
    west_set, west_pairs = sent_along(with_pairs(faces[0], face_places[0]), face_places[0], "gx")
    south_set, south_pairs = sent_along(with_pairs(faces[1], face_places[1]), face_places[1], "gy")

    initial = math.sqrt(2.0) * jnp.cos(phases[:, :, 0])
    field = jnp.stack([initial[..., i * width : (i + 1) * width] for i in range(CHUNKS)])
    layer_fields = [passed_along(field[0], "gz", -1)]
    if layers > 2:
        layer_fields.append(passed_along(field[0], "gz", 1))
    diagonal = diag_tiles.reshape(clusters, degrees, degrees)
    own, east, north = build(
        [
            (clusters, [(0, "both"), (3, "diagonal")]),
            (edge, [(1, "forward")]),
            (edge, [(2, "forward")]),
        ],
        [local_tiles.shape[3], faces.shape[1], faces.shape[1], clusters],
        edge,
        [local_pairs[0, 0, 0], face_places[0], face_places[1], face_places[0]],
        [local_tiles[0, 0, 0], faces[0], faces[1], diagonal],
        6 * 10**7,
    )
    if layers > 2:
        layer_plan = [(clusters, [(0, "forward")]), (clusters, [(1, "reverse")])]
    else:
        layer_plan = [(clusters, [(0, "forward"), (1, "reverse")])]
    *across, west, south = build(
        layer_plan + [(edge, [(2, "reverse")]), (edge, [(3, "reverse")])],
        [own_layer.shape[0], layer_packed.shape[0], faces.shape[1], faces.shape[1]],
        edge,
        [own_layer_pairs, below_pairs, west_pairs, south_pairs],
        [own_layer, below_set, west_set, south_set],
        3 * 10**7,
    )
    normalizer = lax.axis_size("gx") * lax.axis_size("gy") * clusters * degrees
    order_three, moments = recur(
        field,
        layer_fields,
        own,
        across,
        [east, west, north, south],
        (edge, edge, 1, degrees, columns),
        float(normalizer),
    )
    return order_three, moments.transpose(1, 0, 2)


def solution(mesh):
    in_specs = (
        P("gx", "gy", "gz", None, None),
        P("gx", "gy", "gz", None, None),
        P("gx", "gy", "gz", None, None, None),
        P("gx", "gy", "gz", None, None),
        P("gx", "gy", "gz", None, None, None, None),
        P("gx", "gy", "gz", None, None, None),
        P("gx", "gy", "gz", None, None, None),
        P("gx", "gy", "gz", None, None),
    )
    out_specs = (P("gx", "gy", "gz", None, None), P("gz", None, None))
    return jax.shard_map(shards, mesh=mesh, in_specs=in_specs, out_specs=out_specs, check_vma=False)
```

```python
import functools
import math

import jax
import jax.numpy as jnp
from jax import lax
from jax.experimental import pallas as pl
from jax.experimental.pallas import tpu as pltpu
from jax.sharding import PartitionSpec as P

CHUNKS = 2
TOGETHER = 8
PIECES = 2
MESH = pl.DeviceIdType.MESH
VMEM_LIMIT = 60 * 1024 * 1024


def passed_along(block, axis, distance):
    count = lax.axis_size(axis)
    route = [((i - distance) % count, i) for i in range(count)]
    return lax.ppermute(block, axis, route)


def halves(values):
    high = values.astype(jnp.bfloat16)
    return high, (values - high.astype(jnp.float32)).astype(jnp.bfloat16)


def packed(tiles):
    count, degrees, _ = tiles.shape
    spare = -degrees % 128
    if spare == 0 or degrees % spare or count * spare % (128 * TOGETHER) or degrees % 8:
        return tiles
    pieces = degrees // spare
    kept = count * degrees // 128
    last = tiles[kept:].reshape(count - kept, degrees, pieces, spare).transpose(0, 2, 1, 3)
    return jnp.concatenate([tiles[:kept], last.reshape(kept, degrees, spare)], axis=2)


def with_pairs(tiles, pairs):
    _, degrees, lanes = tiles.shape
    spare = ((0, degrees - pairs.shape[0]), (0, lanes - pairs.shape[1]))
    return jnp.concatenate([tiles, jnp.pad(pairs.astype(jnp.float32), spare)[None]])


def sent_along(carried, pairs, axis):
    received = passed_along(carried, axis, 1)
    return received, received[-1, 0:2, 0 : pairs.shape[1]].astype(jnp.int32)


def build_kernel(plan, counts, edge, *refs):
    n_src = 1 + max(source for _, parts in plan for source, _ in parts)
    pairs, tiles = refs[:n_src], refs[n_src : 2 * n_src]
    outs = refs[2 * n_src : 2 * n_src + len(plan)]
    block, wide, turn = refs[2 * n_src + len(plan) :]
    _, degrees, slab = wide.shape
    wide[...] = jnp.zeros_like(wide)
    turn[...] = jnp.zeros_like(turn)

    def place(places):
        for j, (_, _, values) in enumerate(places):
            wide[j, :, 0 : values.shape[1]] = values
        moved = [
            pltpu.roll(wide[j], (column % edge) * degrees, 1)
            for j, (_, column, _) in enumerate(places)
        ]
        for (row, column, _), values in zip(places, moved):
            start = pl.multiple_of((column // edge) * slab, slab)
            block[row, :, pl.ds(start, slab)] += values

    def turned(j, tile):
        for at, piece in tile:
            turn[j, 0:degrees, at : at + piece.shape[1]] = piece
        return turn[j].T[0:degrees]

    for out, (clusters, parts) in zip(outs, plan):
        span = clusters * degrees

        def clear(i, carry):
            block[i, :, 0:span] = jnp.zeros((degrees, span), jnp.float32)
            return carry

        lax.fori_loop(0, clusters, clear, 0)
        for source, kind in parts:
            stored = tiles[source]
            spare = stored.shape[2] - degrees

            def some(step, carry, source=source, kind=kind, stored=stored, first_tile=0, tail=False):
                places = []
                for j in range(TOGETHER):
                    k = step * TOGETHER + j
                    index = first_tile + k
                    if kind == "diagonal":
                        owner, partner = k, k
                    else:
                        owner, partner = pairs[source][0, index], pairs[source][1, index]
                    if tail:
                        pieces = degrees // spare
                        tile = [
                            (i * spare, stored[k * pieces + i][:, degrees:]) for i in range(pieces)
                        ]
                    else:
                        tile = [(0, stored[k][:, 0:degrees])]
                    if kind != "reverse":
                        places.append((owner, partner, tile[0][1]))
                    if kind != "forward":
                        places.append((partner, owner, turned(j, tile)))
                place(places)
                return carry

            count = counts[source]
            lax.fori_loop(0, count // TOGETHER, some, 0)
            if spare:
                rest = functools.partial(some, first_tile=count, tail=True)
                lax.fori_loop(0, count * spare // degrees // TOGETHER, rest, 0)

        def write(i, carry, out=out, span=span):
            high, low = halves(block[i, :, 0:span])
            group, at = i // edge, pl.multiple_of((i % edge) * degrees, degrees)
            out[group, pl.ds(at, degrees), :] = high
            out[group, pl.ds(slab + at, degrees), :] = low
            return carry

        lax.fori_loop(0, clusters, write, 0)


def build(plan, counts, edge, pairs, tiles, cost):
    degrees = tiles[0].shape[1]
    slab = edge * degrees
    most = max(clusters for clusters, _ in plan)
    around = -(-degrees // 128) * 128
    return pl.pallas_call(
        functools.partial(build_kernel, plan, counts, edge),
        out_shape=[
            jax.ShapeDtypeStruct((c // edge, 2 * slab, c * degrees), jnp.bfloat16) for c, _ in plan
        ],
        in_specs=[pl.BlockSpec(memory_space=pltpu.SMEM)] * len(pairs)
        + [pl.BlockSpec(memory_space=pltpu.VMEM)] * len(tiles),
        out_specs=[pl.BlockSpec(memory_space=pltpu.VMEM)] * len(plan),
        scratch_shapes=[
            pltpu.VMEM((most, degrees, most * degrees), jnp.float32),
            pltpu.VMEM((2 * TOGETHER, degrees, slab), jnp.float32),
            pltpu.VMEM((TOGETHER, around, around), jnp.float32),
        ],
        compiler_params=pltpu.CompilerParams(vmem_limit_bytes=VMEM_LIMIT),
        cost_estimate=pl.CostEstimate(flops=250 * cost, bytes_accessed=cost, transcendentals=0),
    )(*pairs, *tiles)


def recur_kernel(layers, width_x, width_y, normalizer, *refs):
    ways = min(layers - 1, 2)
    field0, first_layer = refs[0], refs[1 : 1 + ways]
    refs = refs[1 + ways :]
    stored, refs = refs[: 5 + ways], refs[5 + ways :]
    out, moments, field1, field2, field3, got_layer, got_face, refs = *refs[:7], refs[7:]
    loaded, load_sem, refs = refs[: 5 + ways], refs[5 + ways], refs[6 + ways :]
    own, across, sides = loaded[0], loaded[1 : 1 + ways], loaded[1 + ways :]
    split, split_side, partial, got_y, got_x, send_sem, recv_sem, sum_send, sum_recv = refs
    chunks, edge, _, degrees, width = field0.shape
    slab = edge * degrees
    pieces = PIECES if edge % PIECES == 0 else 1
    fields = [field0, field1, field2, field3]
    me_x, me_y, me_z = lax.axis_index("gx"), lax.axis_index("gy"), lax.axis_index("gz")
    x_peers = [{"gx": lax.rem(me_x + d, width_x)} for d in range(1, width_x)]
    y_peers = [{"gy": lax.rem(me_y + d, width_y)} for d in range(1, width_y)]
    below = {"gz": lax.rem(me_z + layers - 1, layers)}
    above = {"gz": lax.rem(me_z + 1, layers)}
    z_peers = [below, above][:ways]

    loads = [
        pltpu.make_async_copy(source, target, load_sem.at[j])
        for j, (source, target) in enumerate(zip(stored, loaded))
    ]
    for load in loads:
        load.start()
    barrier = pltpu.get_barrier_semaphore()
    for peer in x_peers + y_peers + z_peers:
        pl.semaphore_signal(barrier, inc=1, device_id=peer, device_id_type=MESH)
    pl.semaphore_wait(barrier, len(x_peers) + len(y_peers) + ways)

    def copies(op, ch):
        field = fields[op]
        found = []
        for j in range(ways):
            for p in range(pieces):
                piece = pl.ds(p * (edge // pieces), edge // pieces)
                found.append(
                    (field.at[ch, piece], got_layer.at[op, j, ch, piece], z_peers[j])
                )
        ends = [
            (field.at[ch, 0], x_peers[-1]),
            (field.at[ch, edge - 1], x_peers[0]),
            (field.at[ch, :, 0], y_peers[-1]),
            (field.at[ch, :, edge - 1], y_peers[0]),
        ]
        for j, (source, peer) in enumerate(ends):
            found.append((source, got_face.at[op, j, ch], peer))
        order = found[ways * pieces :] + found[: ways * pieces]
        return [
            pltpu.make_async_remote_copy(
                src_ref=source,
                dst_ref=target,
                send_sem=send_sem.at[op, ch, j],
                recv_sem=recv_sem.at[op, ch, j],
                device_id=peer,
                device_id_type=MESH,
            )
            for j, (source, target, peer) in enumerate(order)
        ]

    def into_split(values, i):
        high, low = halves(values.reshape(slab, width))
        split[pl.ds(pl.multiple_of(i * slab, slab), slab), 0:width] = high
        split[pl.ds(pl.multiple_of(i * slab, slab), slab), width : 2 * width] = low

    def folded(both):
        four = both[0:slab] + both[slab : 2 * slab]
        return four[:, 0:width] + four[:, width : 2 * width]

    def apply(matrix, source, target, ch, fresh, begin, end):
        def fill(i, carry):
            into_split(source(i), i)
            return carry

        lax.fori_loop(begin, end, fill, 0)
        rows = slice(begin * slab, end * slab)

        def part(i, carry):
            both = jnp.dot(matrix[i, :, rows], split[rows], preferred_element_type=jnp.float32)
            value = folded(both).reshape(edge, degrees, width)
            target[ch, i] = value if fresh else target[ch, i] + value
            return carry

        lax.fori_loop(0, edge, part, 0)

    def side(j, values):
        high, low = halves(values.reshape(slab, width))
        split_side[:, 0:width] = high
        split_side[:, width : 2 * width] = low
        both = jnp.dot(sides[j][0], split_side[...], preferred_element_type=jnp.float32)
        return folded(both).reshape(edge, degrees, width)

    def inner(left, right, ch):
        def add(i, total):
            return total + jnp.sum(
                (left[ch, i] * right[ch, i]).reshape(slab, width), axis=0, keepdims=True
            )

        return lax.fori_loop(0, edge, add, jnp.zeros((1, width), jnp.float32))

    for ch in range(chunks):
        for copy in copies(0, ch)[: 4 if ch == 0 else None]:
            copy.start()
    partial[...] = jnp.zeros_like(partial)
    for op in range(3):
        field, target = fields[op], fields[op + 1]

        def step(ch, carry, op=op, field=field, target=target):
            first = op == 0 and isinstance(ch, int) and ch == 0
            if first:
                loads[0].wait()
            apply(own, lambda i: field[ch, i], target, ch, True, 0, edge)
            if first:
                for load in loads[1:]:
                    load.wait()
            arrivals = copies(op, ch)
            for copy in arrivals[:4]:
                copy.wait_recv()
            face = [got_face[op, j, ch] for j in range(4)]
            target[ch, edge - 1] += side(0, face[0])
            target[ch, 0] += side(1, face[1])
            target[ch, :, edge - 1] += side(2, face[2])
            target[ch, :, 0] += side(3, face[3])
            for j in range(ways):
                for p in range(pieces):
                    begin, end = p * (edge // pieces), (p + 1) * (edge // pieces)
                    if first:
                        apply(across[j], lambda i: first_layer[j][i], target, ch, False, begin, end)
                    else:
                        arrivals[4 + j * pieces + p].wait_recv()
                        apply(
                            across[j],
                            lambda i: got_layer[op, j, ch, i],
                            target,
                            ch,
                            False,
                            begin,
                            end,
                        )
            if op > 0:

                def combine(i, carry):
                    target[ch, i] = 2.0 * target[ch, i] - fields[op - 1][ch, i]
                    return carry

                lax.fori_loop(0, edge, combine, 0)
            if op < 2:
                for copy in copies(op + 1, ch):
                    copy.start()
            if op == 0:
                partial[ch, 0:1] = inner(field, field, ch)
            partial[ch, 2 * op + 1 : 2 * op + 2] = inner(target, field, ch)
            partial[ch, 2 * op + 2 : 2 * op + 3] = inner(target, target, ch)
            return carry

        if op == 0:
            for ch in range(chunks):
                step(ch, 0)
        else:
            lax.fori_loop(0, chunks, step, 0)

    def gather(stage, peers, slots):
        sends = [
            pltpu.make_async_remote_copy(
                src_ref=partial.at[:],
                dst_ref=slots.at[d],
                send_sem=sum_send.at[stage, d],
                recv_sem=sum_recv.at[stage, d],
                device_id=peer,
                device_id_type=MESH,
            )
            for d, peer in enumerate(peers)
        ]
        for send in sends:
            send.start()
        return sends

    sends = gather(0, y_peers, got_y)
    for ch in range(chunks):
        out[:, :, 0, :, ch * width : (ch + 1) * width] = field3[ch]
    for send in sends:
        send.wait()
    total = partial[...]
    for d in range(len(y_peers)):
        total = total + got_y[d]
    partial[...] = total
    sends = gather(1, x_peers, got_x)
    for send in sends:
        send.wait()
    total = partial[...]
    for d in range(len(x_peers)):
        total = total + got_x[d]
    total = total * (1.0 / normalizer)
    for ch in range(chunks):
        at = slice(ch * width, (ch + 1) * width)
        for k in range(7):
            row = total[ch, k : k + 1]
            if k > 1:
                row = 2.0 * row - total[ch, k % 2 : k % 2 + 1]
            moments[k, :, at] = row

    for copy in copies(0, 0)[:4]:
        copy.wait_send()
    for op in range(3):

        def finish(ch, carry, op=op):
            for copy in copies(op, ch):
                copy.wait_send()
            return carry

        lax.fori_loop(1 if op == 0 else 0, chunks, finish, 0)


def recur(field, layer_fields, own, across, sides, out_shape, normalizer):
    chunks, edge, _, degrees, width = field.shape
    layers, nx, ny = lax.axis_size("gz"), lax.axis_size("gx"), lax.axis_size("gy")
    ways = len(layer_fields)
    operands = [field, *layer_fields, own, *across, *sides]
    f32 = jnp.float32
    rows = edge * edge * degrees
    return pl.pallas_call(
        functools.partial(recur_kernel, layers, nx, ny, normalizer),
        out_shape=[
            jax.ShapeDtypeStruct(out_shape, f32),
            jax.ShapeDtypeStruct((7, 1, chunks * width), f32),
        ],
        in_specs=[pl.BlockSpec(memory_space=pltpu.VMEM)] * (1 + ways)
        + [pl.BlockSpec(memory_space=pl.ANY)] * (5 + ways),
        out_specs=[pl.BlockSpec(memory_space=pltpu.VMEM)] * 2,
        scratch_shapes=[
            pltpu.VMEM(field.shape, f32),
            pltpu.VMEM(field.shape, f32),
            pltpu.VMEM(field.shape, f32),
            pltpu.VMEM((3, ways) + field.shape, f32),
            pltpu.VMEM((3, 4, chunks, edge, degrees, width), f32),
            *[pltpu.VMEM(matrix.shape, matrix.dtype) for matrix in (own, *across, *sides)],
            pltpu.SemaphoreType.DMA((5 + ways,)),
            pltpu.VMEM((rows, 2 * width), jnp.bfloat16),
            pltpu.VMEM((edge * degrees, 2 * width), jnp.bfloat16),
            pltpu.VMEM((chunks, 8, width), f32),
            pltpu.VMEM((ny - 1, chunks, 8, width), f32),
            pltpu.VMEM((nx - 1, chunks, 8, width), f32),
            pltpu.SemaphoreType.DMA((3, chunks, PIECES * ways + 4)),
            pltpu.SemaphoreType.DMA((3, chunks, PIECES * ways + 4)),
            pltpu.SemaphoreType.DMA((2, max(nx, ny) - 1)),
            pltpu.SemaphoreType.DMA((2, max(nx, ny) - 1)),
        ],
        compiler_params=pltpu.CompilerParams(
            collective_id=0, has_side_effects=True, vmem_limit_bytes=VMEM_LIMIT
        ),
    )(*operands)


def shards(
    phases, diag_tiles, local_tiles, local_pairs, face_tiles, face_pairs, layer_tiles, layer_pairs
):
    edge = phases.shape[0]
    clusters = edge * edge
    degrees, columns = phases.shape[3:]
    layers = lax.axis_size("gz")
    width = columns // CHUNKS

    own_layer, own_layer_pairs = layer_tiles[0, 0, 0], layer_pairs[0, 0, 0]
    faces, face_places = face_tiles[0, 0, 0], face_pairs[0, 0, 0]
    layer_packed = packed(own_layer)
    carried = with_pairs(layer_packed, own_layer_pairs)
    below_set, below_pairs = sent_along(carried, own_layer_pairs, "gz")
    west_set, west_pairs = sent_along(with_pairs(faces[0], face_places[0]), face_places[0], "gx")
    south_set, south_pairs = sent_along(with_pairs(faces[1], face_places[1]), face_places[1], "gy")

    initial = math.sqrt(2.0) * jnp.cos(phases[:, :, 0])
    field = jnp.stack([initial[..., i * width : (i + 1) * width] for i in range(CHUNKS)])
    layer_fields = [passed_along(field[0], "gz", -1)]
    if layers > 2:
        layer_fields.append(passed_along(field[0], "gz", 1))
    diagonal = diag_tiles.reshape(clusters, degrees, degrees)
    own, east, north = build(
        [
            (clusters, [(0, "both"), (3, "diagonal")]),
            (edge, [(1, "forward")]),
            (edge, [(2, "forward")]),
        ],
        [local_tiles.shape[3], faces.shape[1], faces.shape[1], clusters],
        edge,
        [local_pairs[0, 0, 0], face_places[0], face_places[1], face_places[0]],
        [local_tiles[0, 0, 0], faces[0], faces[1], diagonal],
        6 * 10**7,
    )
    if layers > 2:
        layer_plan = [(clusters, [(0, "forward")]), (clusters, [(1, "reverse")])]
    else:
        layer_plan = [(clusters, [(0, "forward"), (1, "reverse")])]
    *across, west, south = build(
        layer_plan + [(edge, [(2, "reverse")]), (edge, [(3, "reverse")])],
        [own_layer.shape[0], layer_packed.shape[0], faces.shape[1], faces.shape[1]],
        edge,
        [own_layer_pairs, below_pairs, west_pairs, south_pairs],
        [own_layer, below_set, west_set, south_set],
        3 * 10**7,
    )
    normalizer = lax.axis_size("gx") * lax.axis_size("gy") * clusters * degrees
    order_three, moments = recur(
        field,
        layer_fields,
        own,
        across,
        [east, west, north, south],
        (edge, edge, 1, degrees, columns),
        float(normalizer),
    )
    return order_three, moments.transpose(1, 0, 2)


def solution(mesh):
    in_specs = (
        P("gx", "gy", "gz", None, None),
        P("gx", "gy", "gz", None, None),
        P("gx", "gy", "gz", None, None, None),
        P("gx", "gy", "gz", None, None),
        P("gx", "gy", "gz", None, None, None, None),
        P("gx", "gy", "gz", None, None, None),
        P("gx", "gy", "gz", None, None, None),
        P("gx", "gy", "gz", None, None),
    )
    out_specs = (P("gx", "gy", "gz", None, None), P("gz", None, None))
    return jax.shard_map(shards, mesh=mesh, in_specs=in_specs, out_specs=out_specs, check_vma=False)
```
